32 devices in a mesh: segment: 2 (over y), fsdp: 4 (over z), seq: 4 (over x, core).
Axes of the slice: x: 2, y: 2, z: 4, core: 2. Of those that a mesh axis runs over, the one named last changes fastest.
Arguments:
- branch_x: bfloat16 [8, 512, 4096], P(('segment', 'fsdp'), 'seq'), may hold values from -6 to 6
- positions: int32 [8, 512], P(('segment', 'fsdp'), 'seq'), may hold values from 0 to 511, as said below
- teacher_held: bfloat16 [8, 512, 4096], P(('segment', 'fsdp'), 'seq'), may hold values from -6 to 6
- gate_weights: bfloat16 [32, 2, 128, 128], P('fsdp'), may hold values from -0.5 to 0.5
- gate_bias: float32 [2, 4096], replicated, may hold values from -4 to 4
- conv_weight: float32 [4, 4096], replicated, may hold values from -3 to 3
- conv_bias: float32 [4096], replicated, may hold values from -3 to 3
- decay_rate: float32 [4096], replicated, as said below
Outputs:
- student_out: bfloat16 [8, 512, 4096], P(('segment', 'fsdp'), 'seq')
- token_loss: float32 [8, 512], P(('segment', 'fsdp'), 'seq')
The draws below stay inside these ranges and needn't reach their ends.
Inputs may be any that keep to these rules, and one draw needn't show every extreme that they name: `positions`: within each sequence a token's position is 0 at a document start and one more than the previous token's position otherwise; every sequence begins with a document start; the first sequence is one whole document. `decay_rate`: rates are positive.
All inputs are finite; a program needn't handle non-finite values.
Results may differ from the reference program's by a relative error of at most 0.0055.
Values may be sent and summed in bfloat16 or wider, within the bound.
No kernel may reach another device: no remote copies, remote signals or barrier semaphores. Data moves between devices by JAX's collectives and lax.ppermute only.
A program may use at most 64 MiB of HBM per device.

```python
import jax
import jax.numpy as jnp
from jax import lax

HEADS = 32
HS = 128
R = 4096
LEN = 512
SEQS = 8


def draw_positions(key, part):
    starts = jax.random.randint(key, (SEQS, LEN), 0, LEN // 4) == 0
    index_row = jnp.arange(LEN, dtype=jnp.int32)[None, :] + jnp.zeros((SEQS, LEN), jnp.int32)
    seq_row = jnp.arange(SEQS, dtype=jnp.int32)[:, None] + jnp.zeros((SEQS, LEN), jnp.int32)
    starts = jnp.logical_and(starts, seq_row != 0)
    starts = jnp.logical_or(starts, index_row == 0)
    marks = jnp.where(starts, index_row, jnp.zeros_like(index_row))
    latest = lax.cummax(marks, axis=1)
    return (index_row - latest).astype(jnp.int32)


def draw_decay_rate(key, part):
    first_key = jax.random.fold_in(key, 11)
    lowest = jnp.log(jnp.float32(0.02))
    highest = jnp.log(jnp.float32(LEN) / 160.0)
    rates = jnp.exp(lowest + jax.random.uniform(first_key, (R,), jnp.float32) * (highest - lowest))
    return rates.astype(jnp.float32)


def block_scale(own_key, dims, pieces, smallest, top_value):
    def one(position, blocks):
        heights = jax.random.uniform(jax.random.fold_in(jax.random.fold_in(own_key, 6), position), (blocks,), jnp.float32, smallest / len(pieces), top_value / len(pieces))
        return jnp.repeat(jnp.exp(heights), dims[position] // blocks).reshape((-1,) + (1,) * (len(dims) - position - 1))

    level = one(*pieces[0])
    for cut in pieces[1:]:
        level = level * one(*cut)
    return level


def normal_values(rng, extent, deviation, reach, cuts=(), held_as=jnp.bfloat16):
    entries = jax.random.normal(rng, extent, jnp.float32) * deviation
    if len(cuts) > 0:
        entries = block_scale(rng, extent, cuts, -0.22, 0.18) * entries
    return jnp.clip(entries, min=-reach, max=reach).astype(held_as)


def setup_inputs(seed: int = 0) -> dict:
    key_list = jax.random.split(jax.random.key(seed), 9)
    branch_x = normal_values(key_list[0], (SEQS, LEN, R), 1.0, 6.0, ((0, 8), (1, 4)))
    positions = draw_positions(jax.random.fold_in(key_list[8], 71), 0)
    teacher_held = normal_values(key_list[2], (SEQS, LEN, R), 1.0, 6.0, ((0, 8), (1, 4)))
    gate_weights = normal_values(key_list[3], (HEADS, 2, HS, HS), HS ** -0.5, 0.5, ((0, 4),))
    gate_bias = normal_values(key_list[4], (2, R), 1.0, 4.0, (), jnp.float32)
    conv_weight = normal_values(key_list[5], (4, R), 4 ** -0.5, 3.0, (), jnp.float32)
    conv_bias = normal_values(key_list[6], (R,), 0.5, 3.0, (), jnp.float32)
    decay_rate = draw_decay_rate(jax.random.fold_in(key_list[8], 71), 0)
    return {"branch_x": branch_x, "positions": positions, "teacher_held": teacher_held, "gate_weights": gate_weights, "gate_bias": gate_bias, "conv_weight": conv_weight, "conv_bias": conv_bias, "decay_rate": decay_rate}


def one_sequence(inputs, gate_weights, gate_bias, conv_weight, conv_bias, decay_rate):
    rows, places, target = inputs
    rows_f = rows.astype(jnp.float32)
    padded = jnp.concatenate([jnp.zeros((3, R), jnp.float32), rows_f], axis=0)
    conv = jnp.zeros((LEN, R), jnp.float32) + conv_bias
    for lag_steps in range(4):
        valid = (places >= lag_steps).astype(jnp.float32)[:, None]
        conv = conv + conv_weight[lag_steps] * padded[3 - lag_steps:3 - lag_steps + LEN] * valid
    conv_rounded = conv.astype(jnp.bfloat16)
    conv_f = conv_rounded.astype(jnp.float32)
    weights_f = gate_weights.astype(jnp.float32)
    preact = jnp.einsum('thi,hgij->thgj', conv_f.reshape(LEN, HEADS, HS), weights_f)
    gate_x = jax.nn.sigmoid(preact[:, :, 0, :].reshape(LEN, R) + gate_bias[0])
    gate_a = jax.nn.sigmoid(preact[:, :, 1, :].reshape(LEN, R) + gate_bias[1])
    log_a = -8.0 * gate_a * decay_rate / LEN
    reset = (places == 0)[:, None]
    decay = jnp.where(reset, jnp.float32(0.0), jnp.exp(log_a))
    scale = jnp.where(reset, jnp.float32(1.0), jnp.sqrt(-jnp.expm1(2.0 * log_a)))
    drive = conv_f * gate_x * scale

    def advance(state, pair):
        state = pair[0] * state + pair[1]
        return (state, state)
    _, states = lax.scan(advance, jnp.zeros((R,), jnp.float32), (decay, drive))
    student = states.astype(jnp.bfloat16)
    student_f = student.astype(jnp.float32)
    normed = student_f * lax.rsqrt(lax.optimization_barrier(jnp.mean(student_f * student_f, axis=-1, keepdims=True)) + 1e-06)
    loss = lax.optimization_barrier(jnp.mean((normed - target.astype(jnp.float32)) ** 2, axis=-1))
    return (student, loss)

def reference(branch_x, positions, teacher_held, gate_weights, gate_bias, conv_weight, conv_bias, decay_rate):
    targets = jnp.roll(teacher_held, -(SEQS // 2), axis=0)

    def apply_one(inputs):
        return one_sequence(inputs, gate_weights, gate_bias, conv_weight, conv_bias, decay_rate)
    student_out, token_loss = lax.map(apply_one, (branch_x, positions, targets))
    return (student_out, token_loss)
```

```python
import functools
import math

import jax
import jax.numpy as jnp
from jax import lax
from jax.experimental import pallas as pl
from jax.experimental.pallas import tpu as pltpu
from jax.sharding import PartitionSpec as P

HEADS = 32
HS = 128
LOG2E = math.log2(math.e)
LN2 = math.log(2.0)
STEPS = 16
EDGE = 16


def prefix(value, axis, combine, identity):
    devices, here = (lax.axis_size(axis), lax.axis_index(axis))
    everything = jax.tree.map(lambda part: lax.all_gather(part, axis), value)
    start = jax.tree.map(
        lambda part, zero: jnp.broadcast_to(jnp.asarray(zero, part.dtype), part.shape),
        value,
        identity,
    )

    def hop(k, before):
        reached = k < here
        new = combine(before, jax.tree.map(lambda part: part[k], everything))
        return jax.tree.map(lambda a, b: jnp.where(reached, a, b), new, before)

    return lax.fori_loop(0, devices, hop, start)


def from_partner(value, axis, apart):
    return lax.ppermute(value, axis, [(i, i ^ 1 << apart) for i in range(lax.axis_size(axis))])


def from_behind(value, axis, steps):
    count = lax.axis_size(axis)
    leading, last = (max(0, -steps), min(count, count - steps))
    return lax.ppermute(value, axis, [(source, source + steps) for source in range(leading, last)])


def combine(former, latter):
    return (former[0] * latter[0], latter[0] * former[1] + latter[1])


def recurrence(conv_rows, gate_pre_x, gate_pre_a, bias_pair, rates, places):
    group = conv_rows.shape[0]
    tokens = conv_rows.shape[1]
    width = conv_rows.shape[2]
    blocks = tokens // 8
    seq_total = lax.axis_size("seq") * tokens
    gate_x = jax.nn.sigmoid(gate_pre_x + bias_pair[0])
    gate_a = jax.nn.sigmoid(gate_pre_a + bias_pair[1])
    log_a = -8.0 * gate_a * rates / seq_total
    reset = (places == 0)[:, :, None]
    decay = jnp.where(reset, jnp.float32(0.0), jnp.exp(log_a))
    scale = jnp.where(reset, jnp.float32(1.0), jnp.sqrt(-jnp.expm1(2.0 * log_a)))
    drive = conv_rows.astype(jnp.float32) * gate_x * scale
    decay_blocks = decay.reshape(group, blocks, 8, width)
    drive_blocks = drive.reshape(group, blocks, 8, width)
    running_prod = jnp.ones((group, blocks, width), jnp.float32)
    running_state = jnp.zeros((group, blocks, width), jnp.float32)
    prod_list = []
    state_list = []
    for inner in range(8):
        step_decay = decay_blocks[:, :, inner, :]
        running_prod = running_prod * step_decay
        running_state = step_decay * running_state + drive_blocks[:, :, inner, :]
        prod_list.append(running_prod)
        state_list.append(running_state)
    block_prod = jnp.swapaxes(running_prod, 0, 1)
    block_state = jnp.swapaxes(running_state, 0, 1)

    def across(carry, pair):
        after = combine(carry, pair)
        return (after, carry)

    start = (jnp.ones((group, width), jnp.float32), jnp.zeros((group, width), jnp.float32))
    ending, befores = lax.scan(across, start, (block_prod, block_state))
    identity = (jnp.ones_like(ending[0]), jnp.zeros_like(ending[1]))
    incoming = prefix(ending, "seq", combine, identity)
    entering = befores[1] + befores[0] * incoming[1][None, :, :]
    entering = jnp.swapaxes(entering, 0, 1)[:, :, None, :]
    products = jnp.stack(prod_list, axis=2)
    local_state = jnp.stack(state_list, axis=2)
    full = local_state + products * entering
    return full.reshape(group, tokens, width).astype(jnp.bfloat16)


def general(
    branch_x, positions, teacher_held, gate_weights, gate_bias, conv_weight, conv_bias, decay_rate
):
    tokens = branch_x.shape[1]
    width = branch_x.shape[2]
    target = from_partner(teacher_held, "segment", 0)
    previous = from_behind(branch_x[:, -3:, :], "seq", 1)
    extended = jnp.concatenate([previous, branch_x], axis=1).astype(jnp.float32)
    conv = jnp.zeros((1, tokens, width), jnp.float32) + conv_bias
    for lag_steps in range(4):
        valid = (positions >= lag_steps).astype(jnp.float32)[:, :, None]
        conv = (
            conv
            + conv_weight[lag_steps]
            * extended[:, 3 - lag_steps : 3 - lag_steps + tokens, :]
            * valid
        )
    conv_rounded = conv.astype(jnp.bfloat16)
    by_heads = conv_rounded.reshape(1, tokens, HEADS, HS)
    preact = jnp.einsum(
        "nthi,hgij->ngthj",
        by_heads,
        lax.all_gather(gate_weights, "fsdp", axis=0, tiled=True),
        preferred_element_type=jnp.float32,
    )
    student = recurrence(
        conv_rounded,
        preact[:, 0].reshape(1, tokens, width),
        preact[:, 1].reshape(1, tokens, width),
        gate_bias,
        decay_rate,
        positions,
    )
    student_f = student.astype(jnp.float32)
    normed = student_f * lax.rsqrt(jnp.mean(student_f * student_f, axis=-1, keepdims=True) + 1e-06)
    token_loss = jnp.mean((normed - target.astype(jnp.float32)) ** 2, axis=-1)
    return (student, token_loss)


def shard_of(shift):
    count = lax.axis_size("fsdp")
    return lax.rem(lax.axis_index("fsdp") + count - shift, count)


def pack_kernel(
    shifts, per, x_ref, pos_ref, w_ref, *refs
):
    devices = lax.axis_size("seq")
    sends, (own_ref, wq_ref, edge_ref), (codes, sem) = refs[:devices], refs[devices : devices + 3], refs[devices + 3 :]
    here = lax.axis_index("seq")
    tokens = x_ref.shape[1]
    shard_heads = w_ref.shape[0]
    shard_width = shard_heads * HS
    wide = per * HS
    copies = []

    def copy(source, target):
        one = pltpu.make_async_copy(source, target, sem.at[len(copies)])
        one.start()
        copies.append(one)

    copy(w_ref.at[pl.ds(here * per, per)], wq_ref)
    own = pl.multiple_of(lax.axis_index("fsdp") * shard_width, shard_width)
    for apart in range(devices - 1, -1, -1):
        owner = lax.bitwise_xor(here, apart)
        for index, shift in enumerate(shifts):
            start = pl.multiple_of((shard_of(shift) * shard_heads + owner * per) * HS, wide)
            copy(
                x_ref.at[0, :, pl.ds(start, wide)],
                sends[apart].at[pl.ds(0, tokens), pl.ds(index * wide, wide)],
            )
    copy(x_ref.at[0, pl.ds(tokens - EDGE, EDGE), pl.ds(own, shard_width)], edge_ref)
    copy(x_ref.at[0, :, pl.ds(own, shard_width)], own_ref)
    coded = jnp.minimum(pos_ref[...], 3).astype(jnp.float32)
    codes[...] = jnp.zeros_like(codes)
    codes[:, :tokens] = jnp.broadcast_to(coded, (EDGE, tokens)).astype(jnp.bfloat16)
    for apart in range(devices):
        copy(codes, sends[apart].at[pl.ds(tokens, EDGE), :])
    for one in copies:
        one.wait()


def pack(branch_x, positions, gate_weights, shifts, per):
    devices = lax.axis_size("seq")
    tokens = branch_x.shape[1]
    width = len(shifts) * per * HS
    shard_width = gate_weights.shape[0] * HS
    send = jax.ShapeDtypeStruct((tokens + EDGE, width), jnp.bfloat16)
    anywhere = pl.BlockSpec(memory_space=pl.ANY)
    out = pl.pallas_call(
        functools.partial(pack_kernel, shifts, per),
        out_shape=[send] * devices
        + [
            jax.ShapeDtypeStruct((tokens, shard_width), jnp.bfloat16),
            jax.ShapeDtypeStruct((per,) + gate_weights.shape[1:], jnp.bfloat16),
            jax.ShapeDtypeStruct((EDGE, shard_width), jnp.bfloat16),
        ],
        in_specs=[anywhere, pl.BlockSpec(memory_space=pltpu.VMEM), anywhere],
        out_specs=[anywhere] * (devices + 3),
        scratch_shapes=[
            pltpu.VMEM((EDGE, width), jnp.bfloat16),
            pltpu.SemaphoreType.DMA((devices * (len(shifts) + 1) + 3,)),
        ],
        compiler_params=pltpu.CompilerParams(vmem_limit_bytes=48 << 20),
        name="pack",
    )(branch_x, positions, gate_weights)
    return out[:devices], out[devices], out[devices + 1], out[devices + 2]


def spread(codes):
    tokens = codes.shape[1]
    down = lax.broadcasted_iota(jnp.int32, (tokens, tokens), 0)
    across = lax.broadcasted_iota(jnp.int32, (tokens, tokens), 1)
    diagonal = jnp.where(down == across, jnp.broadcast_to(codes, (tokens, tokens)), 0.0)
    return jnp.dot(
        diagonal.astype(jnp.bfloat16),
        jnp.ones((tokens, HS), jnp.bfloat16),
        preferred_element_type=jnp.float32,
    )


def write_masks(masks, natural, span):
    for step in range(span):
        code = natural[pl.ds(step, 8, stride=span), :]
        rows = pl.ds(step * 8, 8)
        first = jnp.minimum(code, 1.0)
        masks[0, rows, :] = first
        masks[1, rows, :] = jnp.clip(code - 1.0, 0.0, 1.0)
        masks[2, rows, :] = jnp.clip(code - 2.0, 0.0, 1.0)
        masks[3, rows, :] = jnp.maximum(1.0 - first, 1e-37)


def row_of(ref, index, lanes):
    return ref[pl.ds(index, 1), lanes]


def gated_chunk(rows_ref, tile, first, span, lanes, masks, weights, params, total, carry):
    conv_w, conv_b, bias, rates = params
    tiles = [
        rows_ref[tile, pl.ds(8 + first + step, 8, stride=span), :] for step in range(-3, STEPS)
    ]
    mask_rows = pl.ds(pl.multiple_of(first * 8, 8 * STEPS), 8 * STEPS)
    half = jnp.concatenate(tiles[3:], axis=0) * (row_of(conv_w, 0, lanes) * 0.5) + (
        row_of(conv_b, 0, lanes) * 0.5
    )
    for lag in range(1, 4):
        shifted = jnp.concatenate(tiles[3 - lag : 3 - lag + STEPS], axis=0)
        half = half + shifted * (row_of(conv_w, lag, lanes) * 0.5) * masks[lag - 1, mask_rows, :]
    rounded = half.astype(jnp.bfloat16)
    pre = jnp.dot(rounded, weights, preferred_element_type=jnp.float32)
    gate_x = 1.0 + jnp.tanh(pre[:, :HS] + row_of(bias, 0, lanes) * 0.5)
    gate_a = 1.0 + jnp.tanh(pre[:, HS:] + row_of(bias, 1, lanes) * 0.5)
    power = gate_a * (row_of(rates, 0, lanes) * (-4.0 * LOG2E / total))
    decay = jnp.exp2(power)
    lost = jnp.tanh(power * -LN2)
    square = jnp.maximum(lost + lost * decay * decay, masks[3, mask_rows, :])
    drive = rounded.astype(jnp.float32) * gate_x * (square * lax.rsqrt(square))
    decay = decay * masks[0, mask_rows, :]
    product, state = carry
    states, products = [], []
    for step in range(STEPS):
        at = slice(step * 8, step * 8 + 8)
        state = decay[at] * state + drive[at]
        product = product * decay[at]
        states.append(state)
        products.append(product)
    return jnp.concatenate(states, axis=0), jnp.concatenate(products, axis=0), (product, state)


def across_spans(product, state):
    place = lax.broadcasted_iota(jnp.int32, product.shape, 0)
    for apart in (1, 2, 4):
        reached = place >= apart
        before_p = jnp.where(reached, pltpu.roll(product, apart, 0), 1.0)
        before_s = jnp.where(reached, pltpu.roll(state, apart, 0), 0.0)
        state = product * before_s + state
        product = product * before_p
    enter_p = jnp.where(place >= 1, pltpu.roll(product, 1, 0), 1.0)
    enter_s = jnp.where(place >= 1, pltpu.roll(state, 1, 0), 0.0)
    return product, state, enter_p, enter_s


def own_kernel(
    total, x_ref, edge_ref, pos_ref, w_ref, cw_ref, cb_ref, bias_ref, rate_ref,
    state_ref, prod_ref, enter_ref, end_ref, rows, natural, masks,
):
    tokens, width = x_ref.shape
    span = tokens // 8
    natural[...] = spread(jnp.minimum(pos_ref[...], 3).astype(jnp.float32))
    write_masks(masks, natural, span)
    for tile in range(width // HS):
        column = pl.ds(tile * HS, HS)
        rows[tile, pl.ds(0, 8), :] = edge_ref[:, column].astype(jnp.float32)[EDGE - 8 :]
        rows[tile, pl.ds(8, tokens), :] = x_ref[:, column].astype(jnp.float32)
    base = lax.axis_index("fsdp") * width
    params = (cw_ref, cb_ref, bias_ref, rate_ref)

    def body(head, unused):
        column = pl.ds(pl.multiple_of(head * HS, HS), HS)
        lanes = pl.ds(pl.multiple_of(base + head * HS, HS), HS)
        weights = jnp.concatenate([w_ref[head, 0], w_ref[head, 1]], axis=1)
        carry = (jnp.ones((8, HS), jnp.float32), jnp.zeros((8, HS), jnp.float32))
        for first in range(0, span, STEPS):
            states, products, carry = gated_chunk(
                rows, head, first, span, lanes, masks, weights, params, total, carry
            )
            state_ref[pl.ds(first * 8, 8 * STEPS), column] = states
            prod_ref[pl.ds(first * 8, 8 * STEPS), column] = products
        product, state, enter_p, enter_s = across_spans(*carry)
        enter_ref[0, :, column] = enter_p
        enter_ref[1, :, column] = enter_s
        end_ref[0:1, column] = product[7:8]
        end_ref[1:2, column] = state[7:8]
        return unused

    lax.fori_loop(0, w_ref.shape[0], body, 0, unroll=2)


def in_vmem(count):
    return [pl.BlockSpec(memory_space=pltpu.VMEM)] * count


def own_shard(own_x, edge, positions, gate_weights, params, total):
    tokens, width = own_x.shape
    return pl.pallas_call(
        functools.partial(own_kernel, total),
        out_shape=[
            jax.ShapeDtypeStruct((tokens, width), jnp.float32),
            jax.ShapeDtypeStruct((tokens, width), jnp.float32),
            jax.ShapeDtypeStruct((2, 8, width), jnp.float32),
            jax.ShapeDtypeStruct((2, width), jnp.float32),
        ],
        in_specs=in_vmem(8),
        out_specs=in_vmem(4),
        scratch_shapes=[
            pltpu.VMEM((width // HS, tokens + 8, HS), jnp.float32),
            pltpu.VMEM((tokens, HS), jnp.float32),
            pltpu.VMEM((4, tokens, HS), jnp.float32),
        ],
        compiler_params=pltpu.CompilerParams(vmem_limit_bytes=32 << 20),
        cost_estimate=pl.CostEstimate(
            flops=200 * tokens * width, bytes_accessed=12 * tokens * width, transcendentals=5 * tokens * width
        ),
        name="own_shard",
    )(own_x, edge, positions, gate_weights, *params)


def far_kernel(indices, shifts, per, total, *refs):
    devices = lax.axis_size("seq")
    here = lax.axis_index("seq")
    count = len(indices)
    arrived, refs = refs[:devices], refs[devices:]
    weights_refs, refs = refs[:count], refs[count:]
    params, refs = refs[:4], refs[4:]
    outs, (rows, natural, masks, states_s, prods_s) = refs[:devices], refs[devices:]
    tokens = arrived[0].shape[0] - EDGE
    length = tokens * devices
    span = length // 8
    wide = per * HS
    shard_heads = HEADS // lax.axis_size("fsdp")
    tiles = count * per
    for tile in range(tiles):
        rows[tile, pl.ds(0, 8), :] = jnp.zeros((8, HS), jnp.float32)
    for apart in range(devices):
        owner = lax.bitwise_xor(here, apart)
        place = pl.multiple_of(owner * tokens, tokens)
        for tile in range(tiles):
            slot, head = divmod(tile, per)
            rows[tile, pl.ds(8 + place, tokens), :] = arrived[apart][
                pl.ds(0, tokens), pl.ds(indices[slot] * wide + head * HS, HS)
            ].astype(jnp.float32)
        codes = arrived[apart][pl.ds(tokens, EDGE), pl.ds(0, tokens)].astype(jnp.float32)
        natural[pl.ds(place, tokens), :] = spread(codes[0:1])
    write_masks(masks, natural, span)

    def body(chunk, carries):
        first = pl.multiple_of(chunk * STEPS, STEPS)
        after = []
        for tile in range(tiles):
            slot, head = divmod(tile, per)
            column = pl.ds(tile * HS, HS)
            start = (shard_of(shifts[indices[slot]]) * shard_heads + here * per + head) * HS
            lanes = pl.ds(pl.multiple_of(start, HS), HS)
            weights = jnp.concatenate(
                [weights_refs[slot][head, 0], weights_refs[slot][head, 1]], axis=1
            )
            states, products, carry = gated_chunk(
                rows, tile, first, span, lanes, masks, weights, params, total, carries[tile]
            )
            at = pl.ds(pl.multiple_of(first * 8, 8 * STEPS), 8 * STEPS)
            states_s[at, column] = states
            prods_s[at, column] = products
            after.append(carry)
        return tuple(after)

    begin = (jnp.ones((8, HS), jnp.float32), jnp.zeros((8, HS), jnp.float32))
    carries = lax.fori_loop(0, span // STEPS, body, (begin,) * tiles)
    entering = [across_spans(*carry)[3] for carry in carries]
    for tile in range(tiles):
        column = pl.ds(tile * HS, HS)
        for step in range(span):
            at = pl.ds(step * 8, 8)
            rows[tile, pl.ds(step, 8, stride=span), :] = (
                states_s[at, column] + prods_s[at, column] * entering[tile]
            )
    for apart in range(devices):
        owner = lax.bitwise_xor(here, apart)
        place = pl.multiple_of(owner * tokens, tokens)
        for tile in range(tiles):
            outs[apart][:, pl.ds(tile * HS, HS)] = rows[tile, pl.ds(place, tokens), :].astype(
                jnp.bfloat16
            )


def far_shards(indices, shifts, per, arrived, weights, params, total):
    devices = lax.axis_size("seq")
    tokens = arrived[0].shape[0] - EDGE
    length = tokens * devices
    width = len(indices) * per * HS
    return pl.pallas_call(
        functools.partial(far_kernel, indices, shifts, per, total),
        out_shape=[jax.ShapeDtypeStruct((tokens, width), jnp.bfloat16)] * devices,
        in_specs=in_vmem(devices + len(indices) + 4),
        out_specs=in_vmem(devices),
        scratch_shapes=[
            pltpu.VMEM((width // HS, length + 8, HS), jnp.float32),
            pltpu.VMEM((length, HS), jnp.float32),
            pltpu.VMEM((4, length, HS), jnp.float32),
            pltpu.VMEM((length, width), jnp.float32),
            pltpu.VMEM((length, width), jnp.float32),
        ],
        compiler_params=pltpu.CompilerParams(vmem_limit_bytes=32 << 20),
        cost_estimate=pl.CostEstimate(
            flops=200 * length * width, bytes_accessed=8 * length * width, transcendentals=5 * length * width
        ),
        name="far_shards",
    )(*arrived, *weights, *params)


def student_kernel(batches, shifts, per, *refs):
    devices = lax.axis_size("seq")
    here = lax.axis_index("seq")
    state_ref, prod_ref, enter_ref = refs[:3]
    ends, refs = refs[3 : 3 + devices], refs[3 + devices :]
    pieces, refs = refs[: len(batches) * devices], refs[len(batches) * devices :]
    out_ref, scale_ref, ends_s, natural = refs
    tokens, width = state_ref.shape
    span = tokens // 8
    wide = per * HS
    shard_heads = width // HS
    for apart in range(devices):
        ends_s[lax.bitwise_xor(here, apart)] = ends[apart][...]
    incoming = jnp.zeros((1, width), jnp.float32)
    for place in range(devices - 1):
        after = ends_s[place, 0:1, :] * incoming + ends_s[place, 1:2, :]
        incoming = jnp.where(place < here, after, incoming)
    entering = enter_ref[1] + enter_ref[0] * incoming
    for tile in range(shard_heads):
        column = slice(tile * HS, (tile + 1) * HS)
        for step in range(span):
            at = pl.ds(step * 8, 8)
            natural[tile, pl.ds(step, 8, stride=span), :] = (
                state_ref[at, column] + prod_ref[at, column] * entering[:, column]
            )
    squares = jnp.zeros((tokens, HS), jnp.float32)

    def add(squares, rounded):
        value = rounded.astype(jnp.float32)
        for tile in range(value.shape[1] // HS):
            part = value[:, tile * HS : (tile + 1) * HS]
            squares = squares + part * part
        return squares

    base = pl.multiple_of(lax.axis_index("fsdp") * width, width)
    for tile in range(shard_heads):
        rounded = natural[tile].astype(jnp.bfloat16)
        out_ref[0, :, pl.ds(pl.multiple_of(base + tile * HS, HS), HS)] = rounded
        squares = add(squares, rounded)
    for number, batch in enumerate(batches):
        for slot, index in enumerate(batch):
            shard = shard_of(shifts[index])
            for apart in range(devices):
                owner = lax.bitwise_xor(here, apart)
                rounded = pieces[number * devices + apart][:, slot * wide : (slot + 1) * wide]
                start = pl.multiple_of((shard * shard_heads + owner * per) * HS, wide)
                out_ref[0, :, pl.ds(start, wide)] = rounded
                squares = add(squares, rounded)
    mean = jnp.sum(squares, axis=1, keepdims=True) * (1.0 / out_ref.shape[2])
    scale_ref[...] = jnp.broadcast_to(lax.rsqrt(mean + 1e-06), (tokens, HS))


def student_rows(states, products, enter, ends, batches, shifts, per, pieces):
    devices = lax.axis_size("seq")
    tokens, width = states.shape
    full = HEADS * HS
    flat = [piece for batch in pieces for piece in batch]
    return pl.pallas_call(
        functools.partial(student_kernel, batches, shifts, per),
        out_shape=[
            jax.ShapeDtypeStruct((1, tokens, full), jnp.bfloat16),
            jax.ShapeDtypeStruct((tokens, HS), jnp.float32),
        ],
        in_specs=in_vmem(3 + devices + len(flat)),
        out_specs=in_vmem(2),
        scratch_shapes=[
            pltpu.VMEM((devices, 2, width), jnp.float32),
            pltpu.VMEM((width // HS, tokens, HS), jnp.float32),
        ],
        compiler_params=pltpu.CompilerParams(vmem_limit_bytes=32 << 20),
        cost_estimate=pl.CostEstimate(
            flops=8 * tokens * full, bytes_accessed=6 * tokens * full, transcendentals=0
        ),
        name="student_rows",
    )(states, products, enter, *ends, *flat)


def loss_kernel(student_ref, scale_ref, target_ref, loss_ref):
    tokens = student_ref.shape[1]
    width = student_ref.shape[2]
    scale = scale_ref[...]
    total = jnp.zeros((tokens, HS), jnp.float32)
    for start in range(0, width, HS):
        lanes = slice(start, start + HS)
        off = student_ref[0, :, lanes].astype(jnp.float32) * scale - target_ref[
            0, :, lanes
        ].astype(jnp.float32)
        total = total + off * off
    loss_ref[...] = jnp.sum(total.T, axis=0, keepdims=True) * (1.0 / width)


def token_losses(student, scale, target):
    tokens = student.shape[1]
    return pl.pallas_call(
        loss_kernel,
        out_shape=jax.ShapeDtypeStruct((1, tokens), jnp.float32),
        in_specs=in_vmem(3),
        out_specs=pl.BlockSpec(memory_space=pltpu.VMEM),
        compiler_params=pltpu.CompilerParams(vmem_limit_bytes=32 << 20),
        cost_estimate=pl.CostEstimate(
            flops=4 * student.size, bytes_accessed=4 * student.size, transcendentals=0
        ),
        name="token_losses",
    )(student, scale, target)


def across_seq(value, apart):
    return lax.ppermute(value, "seq", [(i, i ^ apart) for i in range(lax.axis_size("seq"))])


def local(
    branch_x, positions, teacher_held, gate_weights, gate_bias, conv_weight, conv_bias, decay_rate
):
    devices, shards = lax.axis_size("seq"), lax.axis_size("fsdp")
    tokens, width = branch_x.shape[1:]
    total = devices * tokens
    per = gate_weights.shape[0] // devices
    shifts = (1, 3, 2)
    batches = ((0, 1), (2,))
    target = from_partner(teacher_held, "segment", 0)
    sends, own_x, weights_part, edge = pack(branch_x, positions, gate_weights, shifts, per)
    arrived = [sends[0]] + [None] * (devices - 1)
    for apart in range(devices - 1, 0, -1):
        arrived[apart] = across_seq(sends[apart], apart)
    weights = [
        lax.ppermute(weights_part, "fsdp", [(i, (i + shift) % shards) for i in range(shards)])
        for shift in shifts
    ]
    edge = from_behind(edge, "seq", 1)
    params = (
        conv_weight,
        conv_bias.reshape(1, width),
        gate_bias,
        decay_rate.reshape(1, width),
    )
    states, products, enter, end = own_shard(own_x, edge, positions, gate_weights, params, total)
    ends = [end] + [across_seq(end, apart) for apart in range(1, devices)]
    pieces = []
    for batch in batches:
        outs = far_shards(
            batch, shifts, per, arrived, [weights[index] for index in batch], params, total
        )
        pieces.append([outs[0]] + [across_seq(outs[apart], apart) for apart in range(1, devices)])
    student, scale = student_rows(states, products, enter, ends, batches, shifts, per, pieces)
    return student, token_losses(student, scale, target)


def solution(mesh):
    shards, devices = mesh.shape["fsdp"], mesh.shape["seq"]
    held = HEADS // shards
    whole = HEADS % shards == 0 and shards == 4 and held % devices == 0 and devices & (devices - 1) == 0
    in_specs = (
        P(("segment", "fsdp"), "seq", None),
        P(("segment", "fsdp"), "seq"),
        P(("segment", "fsdp"), "seq", None),
        P("fsdp", None, None, None),
        P(),
        P(),
        P(),
        P(),
    )
    out_specs = (P(("segment", "fsdp"), "seq", None), P(("segment", "fsdp"), "seq"))
    return jax.shard_map(
        local if whole else general,
        mesh=mesh,
        in_specs=in_specs,
        out_specs=out_specs,
        check_vma=False,
    )
```

```python
import functools
import math

import jax
import jax.numpy as jnp
from jax import lax
from jax.experimental import pallas as pl
from jax.experimental.pallas import tpu as pltpu
from jax.sharding import PartitionSpec as P

HEADS = 32
HS = 128
LOG2E = math.log2(math.e)
LN2 = math.log(2.0)
EDGE = 16


def prefix(value, axis, combine, identity):
    devices, here = (lax.axis_size(axis), lax.axis_index(axis))
    everything = jax.tree.map(lambda part: lax.all_gather(part, axis), value)
    start = jax.tree.map(
        lambda part, zero: jnp.broadcast_to(jnp.asarray(zero, part.dtype), part.shape),
        value,
        identity,
    )

    def hop(k, before):
        reached = k < here
        new = combine(before, jax.tree.map(lambda part: part[k], everything))
        return jax.tree.map(lambda a, b: jnp.where(reached, a, b), new, before)

    return lax.fori_loop(0, devices, hop, start)


def from_partner(value, axis, apart):
    return lax.ppermute(value, axis, [(i, i ^ 1 << apart) for i in range(lax.axis_size(axis))])


def from_behind(value, axis, steps):
    count = lax.axis_size(axis)
    leading, last = (max(0, -steps), min(count, count - steps))
    return lax.ppermute(value, axis, [(source, source + steps) for source in range(leading, last)])


def combine(former, latter):
    return (former[0] * latter[0], latter[0] * former[1] + latter[1])


def recurrence(conv_rows, gate_pre_x, gate_pre_a, bias_pair, rates, places):
    group = conv_rows.shape[0]
    tokens = conv_rows.shape[1]
    width = conv_rows.shape[2]
    blocks = tokens // 8
    seq_total = lax.axis_size("seq") * tokens
    gate_x = jax.nn.sigmoid(gate_pre_x + bias_pair[0])
    gate_a = jax.nn.sigmoid(gate_pre_a + bias_pair[1])
    log_a = -8.0 * gate_a * rates / seq_total
    reset = (places == 0)[:, :, None]
    decay = jnp.where(reset, jnp.float32(0.0), jnp.exp(log_a))
    scale = jnp.where(reset, jnp.float32(1.0), jnp.sqrt(-jnp.expm1(2.0 * log_a)))
    drive = conv_rows.astype(jnp.float32) * gate_x * scale
    decay_blocks = decay.reshape(group, blocks, 8, width)
    drive_blocks = drive.reshape(group, blocks, 8, width)
    running_prod = jnp.ones((group, blocks, width), jnp.float32)
    running_state = jnp.zeros((group, blocks, width), jnp.float32)
    prod_list = []
    state_list = []
    for inner in range(8):
        step_decay = decay_blocks[:, :, inner, :]
        running_prod = running_prod * step_decay
        running_state = step_decay * running_state + drive_blocks[:, :, inner, :]
        prod_list.append(running_prod)
        state_list.append(running_state)
    block_prod = jnp.swapaxes(running_prod, 0, 1)
    block_state = jnp.swapaxes(running_state, 0, 1)

    def across(carry, pair):
        after = combine(carry, pair)
        return (after, carry)

    start = (jnp.ones((group, width), jnp.float32), jnp.zeros((group, width), jnp.float32))
    ending, befores = lax.scan(across, start, (block_prod, block_state))
    identity = (jnp.ones_like(ending[0]), jnp.zeros_like(ending[1]))
    incoming = prefix(ending, "seq", combine, identity)
    entering = befores[1] + befores[0] * incoming[1][None, :, :]
    entering = jnp.swapaxes(entering, 0, 1)[:, :, None, :]
    products = jnp.stack(prod_list, axis=2)
    local_state = jnp.stack(state_list, axis=2)
    full = local_state + products * entering
    return full.reshape(group, tokens, width).astype(jnp.bfloat16)


def general(
    branch_x, positions, teacher_held, gate_weights, gate_bias, conv_weight, conv_bias, decay_rate
):
    tokens = branch_x.shape[1]
    width = branch_x.shape[2]
    target = from_partner(teacher_held, "segment", 0)
    previous = from_behind(branch_x[:, -3:, :], "seq", 1)
    extended = jnp.concatenate([previous, branch_x], axis=1).astype(jnp.float32)
    conv = jnp.zeros((1, tokens, width), jnp.float32) + conv_bias
    for lag_steps in range(4):
        valid = (positions >= lag_steps).astype(jnp.float32)[:, :, None]
        conv = (
            conv
            + conv_weight[lag_steps]
            * extended[:, 3 - lag_steps : 3 - lag_steps + tokens, :]
            * valid
        )
    conv_rounded = conv.astype(jnp.bfloat16)
    by_heads = conv_rounded.reshape(1, tokens, HEADS, HS)
    preact = jnp.einsum(
        "nthi,hgij->ngthj",
        by_heads,
        lax.all_gather(gate_weights, "fsdp", axis=0, tiled=True),
        preferred_element_type=jnp.float32,
    )
    student = recurrence(
        conv_rounded,
        preact[:, 0].reshape(1, tokens, width),
        preact[:, 1].reshape(1, tokens, width),
        gate_bias,
        decay_rate,
        positions,
    )
    student_f = student.astype(jnp.float32)
    normed = student_f * lax.rsqrt(jnp.mean(student_f * student_f, axis=-1, keepdims=True) + 1e-06)
    token_loss = jnp.mean((normed - target.astype(jnp.float32)) ** 2, axis=-1)
    return (student, token_loss)


def in_vmem(count):
    return [pl.BlockSpec(memory_space=pltpu.VMEM)] * count


def pallas(kernel, name, out_shape, in_specs, out_specs, scratch_shapes, work, **more):
    return pl.pallas_call(
        kernel,
        out_shape=out_shape,
        in_specs=in_specs,
        out_specs=out_specs,
        scratch_shapes=scratch_shapes,
        compiler_params=pltpu.CompilerParams(vmem_limit_bytes=24 << 20),
        cost_estimate=pl.CostEstimate(
            flops=0, bytes_accessed=0, transcendentals=0
        ),
        name=name,
        **more,
    )


def cut_kernel(x_ref, w_ref, half_ref, quarter_ref, edge_ref, sem):
    here = lax.axis_index("seq")
    tokens = x_ref.shape[1]
    halves, quarters = half_ref.shape[0], quarter_ref.shape[0]
    copies = [
        pltpu.make_async_copy(
            w_ref.at[pl.ds(lax.rem(here, 2) * halves, halves)], half_ref, sem.at[0]
        ),
        pltpu.make_async_copy(w_ref.at[pl.ds(here * quarters, quarters)], quarter_ref, sem.at[1]),
        pltpu.make_async_copy(x_ref.at[0, pl.ds(tokens - EDGE, EDGE), :], edge_ref, sem.at[2]),
    ]
    for copy in copies:
        copy.start()
    for copy in copies:
        copy.wait()


def cut(branch_x, gate_weights):
    held = gate_weights.shape[0]
    rest = gate_weights.shape[1:]
    return pallas(
        cut_kernel,
        "cut",
        [
            jax.ShapeDtypeStruct((held // 2,) + rest, jnp.bfloat16),
            jax.ShapeDtypeStruct((held // 4,) + rest, jnp.bfloat16),
            jax.ShapeDtypeStruct((EDGE, branch_x.shape[2]), jnp.bfloat16),
        ],
        [pl.BlockSpec(memory_space=pltpu.HBM)] * 2,
        [pl.BlockSpec(memory_space=pl.ANY)] * 3,
        [pltpu.SemaphoreType.DMA((3,))],
        10000,
    )(
        pltpu.with_memory_space_constraint(branch_x, pltpu.HBM),
        pltpu.with_memory_space_constraint(gate_weights, pltpu.HBM),
    )


def spread(codes):
    tokens = codes.shape[1]
    down = lax.broadcasted_iota(jnp.int32, (tokens, tokens), 0)
    across = lax.broadcasted_iota(jnp.int32, (tokens, tokens), 1)
    diagonal = jnp.where(down == across, jnp.broadcast_to(codes, (tokens, tokens)), 0.0)
    return jnp.dot(
        diagonal.astype(jnp.bfloat16),
        jnp.ones((tokens, HS), jnp.bfloat16),
        preferred_element_type=jnp.float32,
    )


def lanes_of(head):
    return pl.ds(pl.multiple_of(head * HS, HS), HS)


def conv_kernel(x_ref, edge_ref, pos_ref, w_ref, b_ref, out_ref, mask_ref, rows, natural, lags):
    tokens = x_ref.shape[1]
    span = tokens // 8
    natural[...] = spread(jnp.minimum(pos_ref[...], 3).astype(jnp.float32))
    for step in range(span):
        code = natural[pl.ds(step, 8, stride=span), :]
        at = pl.ds(step * 8, 8)
        first = jnp.minimum(code, 1.0)
        mask_ref[0, at, :] = first
        mask_ref[1, at, :] = jnp.maximum(1.0 - first, 1e-37)
        lags[0, at, :] = jnp.clip(code - 1.0, 0.0, 1.0)
        lags[1, at, :] = jnp.clip(code - 2.0, 0.0, 1.0)

    def body(head, unused):
        lanes = lanes_of(head)
        rows[head, pl.ds(0, 8), :] = edge_ref[:, lanes].astype(jnp.float32)[EDGE - 8 :]
        rows[head, pl.ds(8, tokens), :] = x_ref[0, :, lanes].astype(jnp.float32)
        tiles = [rows[head, pl.ds(8 + step, 8, stride=span), :] for step in range(-3, span)]
        half = jnp.concatenate(tiles[3:], axis=0) * (w_ref[0:1, lanes] * 0.5) + (
            b_ref[0:1, lanes] * 0.5
        )
        for lag in range(1, 4):
            shifted = jnp.concatenate(tiles[3 - lag : 3 - lag + span], axis=0)
            mask = mask_ref[0] if lag == 1 else lags[lag - 2]
            half = half + shifted * (w_ref[lag : lag + 1, lanes] * 0.5) * mask
        out_ref[head] = half.astype(jnp.bfloat16)
        return unused

    lax.fori_loop(0, out_ref.shape[0], body, 0, unroll=4)


def conv_rows(branch_x, edge, positions, weight, bias):
    tokens, width = branch_x.shape[1:]
    heads = width // HS
    return pallas(
        conv_kernel,
        "conv_rows",
        [
            jax.ShapeDtypeStruct((heads, tokens, HS), jnp.bfloat16),
            jax.ShapeDtypeStruct((2, tokens, HS), jnp.float32),
        ],
        in_vmem(5),
        in_vmem(2),
        [
            pltpu.VMEM((heads, tokens + 8, HS), jnp.float32),
            pltpu.VMEM((tokens, HS), jnp.float32),
            pltpu.VMEM((2, tokens, HS), jnp.float32),
        ],
        tokens * width,
    )(branch_x, edge, positions, weight, bias)


def across_spans(product, state):
    place = lax.broadcasted_iota(jnp.int32, product.shape, 0)
    for apart in (1, 2, 4):
        reached = place >= apart
        before_p = jnp.where(reached, pltpu.roll(product, apart, 0), 1.0)
        before_s = jnp.where(reached, pltpu.roll(state, apart, 0), 0.0)
        state = product * before_s + state
        product = product * before_p
    enter_p = jnp.where(place >= 1, pltpu.roll(product, 1, 0), 1.0)
    enter_s = jnp.where(place >= 1, pltpu.roll(state, 1, 0), 0.0)
    return product, state, enter_p, enter_s


def shard_kernel(total, pair, counts, earlier, conv_ref, mask_ref, bias_ref, rate_ref, *refs):
    weights, refs = refs[: len(counts)], refs[len(counts) :]
    before, (state_ref, prod_ref, enter_ref, end_ref) = refs[:earlier], refs[earlier:]
    shard_heads, tokens = state_ref.shape[:2]
    span = tokens // 8
    base = lax.bitwise_xor(lax.axis_index("fsdp"), pair) * shard_heads
    here = lax.axis_index("seq") if len(counts) == 4 else lax.rem(lax.axis_index("seq"), 2)
    for slot, ref in enumerate(before):
        end_ref[2 * slot : 2 * slot + 2, :] = ref[...]

    def one(place, weights_of):
        head = base + place
        lanes = lanes_of(head)
        rounded = conv_ref[head]
        pre = jnp.dot(rounded, weights_of, preferred_element_type=jnp.float32)
        gate_x = 1.0 + jnp.tanh(pre[:, :HS] + bias_ref[0:1, lanes] * 0.5)
        gate_a = 1.0 + jnp.tanh(pre[:, HS:] + bias_ref[1:2, lanes] * 0.5)
        power = gate_a * (rate_ref[0:1, lanes] * (-4.0 * LOG2E / total))
        decay = jnp.exp2(power)
        lost = jnp.tanh(power * -LN2)
        square = jnp.maximum(lost + lost * decay * decay, mask_ref[1])
        drive = rounded.astype(jnp.float32) * gate_x * (square * lax.rsqrt(square))
        decay = decay * mask_ref[0]
        product, state = jnp.ones((8, HS), jnp.float32), jnp.zeros((8, HS), jnp.float32)
        for step in range(span):
            at = slice(step * 8, step * 8 + 8)
            state = decay[at] * state + drive[at]
            product = product * decay[at]
            state_ref[place, at, :] = state
            prod_ref[place, at, :] = product
        product, state, enter_p, enter_s = across_spans(product, state)
        enter_ref[place, 0] = enter_p
        enter_ref[place, 1] = enter_s
        row = 2 * earlier
        end_ref[row : row + 1, lanes_of(place)] = product[7:8]
        end_ref[row + 1 : row + 2, lanes_of(place)] = state[7:8]

    for apart, (count, ref) in enumerate(zip(counts, weights)):
        first = lax.bitwise_xor(here, apart) * count if len(counts) > 1 else 0
        for head in range(count):
            one(first + head, jnp.concatenate([ref[head, 0], ref[head, 1]], axis=1))


def shard(conv, masks, params, pair, weights, total, before=()):
    tokens = conv.shape[1]
    counts = tuple(part.shape[0] for part in weights)
    heads = sum(counts)
    return pallas(
        functools.partial(shard_kernel, total, pair, counts, len(before)),
        "shard",
        [
            jax.ShapeDtypeStruct((heads, tokens, HS), jnp.float32),
            jax.ShapeDtypeStruct((heads, tokens, HS), jnp.float32),
            jax.ShapeDtypeStruct((heads, 2, 8, HS), jnp.float32),
            jax.ShapeDtypeStruct((2 * len(before) + 2, heads * HS), jnp.float32),
        ],
        in_vmem(4 + len(weights) + len(before)),
        in_vmem(4),
        [],
        heads * tokens * HS,
    )(conv, masks, *params, *weights, *before)


def rows_kernel(pairs, *refs):
    devices = lax.axis_size("seq")
    here = lax.axis_index("seq")
    ends, refs = refs[:devices], refs[devices:]
    parts = [refs[3 * slot : 3 * slot + 3] for slot in range(len(pairs))]
    student_ref, held_ref, scale_ref, ends_s, natural, sem = refs[3 * len(pairs) :]
    heads, tokens = parts[0][0].shape[:2]
    span = tokens // 8
    width = heads * HS
    for apart in range(devices):
        ends_s[lax.bitwise_xor(here, apart)] = ends[apart][...]
    squares = jnp.zeros((tokens, HS), jnp.float32)
    copies = []
    for slot, (pair, (state_ref, prod_ref, enter_ref)) in enumerate(zip(pairs, parts)):
        incoming = jnp.zeros((1, width), jnp.float32)
        for place in range(devices - 1):
            after = ends_s[place, 2 * slot : 2 * slot + 1, :] * incoming + (
                ends_s[place, 2 * slot + 1 : 2 * slot + 2, :]
            )
            incoming = jnp.where(place < here, after, incoming)
        base = lax.bitwise_xor(lax.axis_index("fsdp"), pair) * heads
        for head in range(heads):
            entering = enter_ref[head, 1] + enter_ref[head, 0] * (
                incoming[:, head * HS : (head + 1) * HS]
            )
            for step in range(span):
                at = slice(step * 8, step * 8 + 8)
                natural[slot * heads + head, pl.ds(step, 8, stride=span), :] = (
                    state_ref[head, at, :] + prod_ref[head, at, :] * entering
                )
            rounded = natural[slot * heads + head].astype(jnp.bfloat16)
            held_ref[0, :, lanes_of(base + head)] = rounded
            value = rounded.astype(jnp.float32)
            squares = squares + value * value
        columns = pl.ds(pl.multiple_of(base * HS, width), width)
        copies.append(
            pltpu.make_async_copy(
                held_ref.at[:, :, columns], student_ref.at[:, :, columns], sem.at[slot]
            )
        )
        copies[-1].start()
    mean = jnp.sum(squares, axis=1, keepdims=True) * (1.0 / student_ref.shape[2])
    scale_ref[...] = jnp.broadcast_to(lax.rsqrt(mean + 1e-06), (tokens, HS))
    for copy in copies:
        copy.wait()


def student_rows(pairs, ends, parts):
    heads, tokens = parts[0][0].shape[:2]
    full = HEADS * HS
    flat = [array for part in parts for array in part[:3]]
    whole = jax.ShapeDtypeStruct((1, tokens, full), jnp.bfloat16)
    return pallas(
        functools.partial(rows_kernel, pairs),
        "student_rows",
        [whole, whole, jax.ShapeDtypeStruct((tokens, HS), jnp.float32)],
        in_vmem(len(ends) + len(flat)),
        [pl.BlockSpec(memory_space=pltpu.HBM)] + in_vmem(2),
        [
            pltpu.VMEM((len(ends),) + ends[0].shape, jnp.float32),
            pltpu.VMEM((HEADS, tokens, HS), jnp.float32),
            pltpu.SemaphoreType.DMA((len(pairs),)),
        ],
        tokens * full,
    )(*ends, *flat)


def loss_kernel(student_ref, scale_ref, target_ref, loss_ref):
    tokens, width = student_ref.shape[1:]
    scale = scale_ref[...]
    total = jnp.zeros((tokens, HS), jnp.float32)
    for start in range(0, width, HS):
        lanes = slice(start, start + HS)
        wanted = target_ref[0, :, lanes].astype(jnp.float32)
        off = student_ref[0, :, lanes].astype(jnp.float32) * scale - wanted
        total = total + off * off
    loss_ref[...] = jnp.sum(total.T, axis=0, keepdims=True) * (1.0 / width)


def token_losses(student, scale, target):
    return pallas(
        loss_kernel,
        "token_losses",
        jax.ShapeDtypeStruct((1, student.shape[1]), jnp.float32),
        in_vmem(3),
        pl.BlockSpec(memory_space=pltpu.VMEM),
        [],
        student.size,
    )(student, scale, target)


def swap(value, axis, apart):
    return lax.ppermute(value, axis, [(i, i ^ apart) for i in range(lax.axis_size(axis))])


def after(value, *earlier):
    return lax.optimization_barrier((value, *earlier))[0]


def local(
    branch_x, positions, teacher_held, gate_weights, gate_bias, conv_weight, conv_bias, decay_rate
):
    tokens, width = branch_x.shape[1:]
    total = lax.axis_size("seq") * tokens
    target = swap(teacher_held, "segment", 1)
    half, quarter, edge = cut(branch_x, gate_weights)
    quarters = {2: swap(quarter, "fsdp", 2)}
    quarters[3] = swap(quarter, "fsdp", 3)
    half = swap(half, "fsdp", 1)
    edge = from_behind(edge, "seq", 1)
    edge = edge
    conv, masks = conv_rows(branch_x, edge, positions, conv_weight, conv_bias.reshape(1, width))
    params = (gate_bias, decay_rate.reshape(1, width))
    pairs = (0, 1, 2, 3)
    parts = {0: shard(conv, masks, params, 0, [gate_weights], total)}

    two = swap(quarters[2], "seq", 2)
    three = swap(after(quarters[3], masks), "seq", 2)
    mine = after(quarters[2], two, parts[0][3])
    weights = [mine, swap(mine, "seq", 1), two, swap(two, "seq", 1)]
    parts[2] = shard(conv, masks, params, 2, weights, total)
    half = after(half,two)
    parts[1] = shard(conv, masks, params, 1, [half, swap(half, "seq", 1)], total)
    mine = after(quarters[3],three)
    weights = [mine, swap(mine, "seq", 1), three, swap(three, "seq", 1)]
    parts[3] = shard(conv, masks, params, 3, weights, total, [parts[pair][3] for pair in pairs[:3]])
    parts = [parts[pair] for pair in pairs]
    end = parts[-1][3]
    ends = [end] + [swap(end, "seq", apart) for apart in (1, 2, 3)]
    student, held, scale = student_rows(pairs, ends, parts)
    return student, token_losses(held, scale, target)


def solution(mesh):
    shards, devices = mesh.shape["fsdp"], mesh.shape["seq"]
    whole = shards == 4 and devices == 4
    in_specs = (
        P(("segment", "fsdp"), "seq", None),
        P(("segment", "fsdp"), "seq"),
        P(("segment", "fsdp"), "seq", None),
        P("fsdp", None, None, None),
        P(),
        P(),
        P(),
        P(),
    )
    out_specs = (P(("segment", "fsdp"), "seq", None), P(("segment", "fsdp"), "seq"))
    return jax.shard_map(
        local if whole else general,
        mesh=mesh,
        in_specs=in_specs,
        out_specs=out_specs,
        check_vma=False,
    )
```

```python
import functools
import math

import jax
import jax.numpy as jnp
from jax import lax
from jax.experimental import pallas as pl
from jax.experimental.pallas import tpu as pltpu
from jax.sharding import PartitionSpec as P

HEADS = 32
HS = 128
LOG2E = math.log2(math.e)
LN2 = math.log(2.0)
EDGE = 16


def prefix(value, axis, combine, identity):
    devices, here = (lax.axis_size(axis), lax.axis_index(axis))
    everything = jax.tree.map(lambda part: lax.all_gather(part, axis), value)
    start = jax.tree.map(
        lambda part, zero: jnp.broadcast_to(jnp.asarray(zero, part.dtype), part.shape),
        value,
        identity,
    )

    def hop(k, before):
        reached = k < here
        new = combine(before, jax.tree.map(lambda part: part[k], everything))
        return jax.tree.map(lambda a, b: jnp.where(reached, a, b), new, before)

    return lax.fori_loop(0, devices, hop, start)


def from_partner(value, axis, apart):
    return lax.ppermute(value, axis, [(i, i ^ 1 << apart) for i in range(lax.axis_size(axis))])


def from_behind(value, axis, steps):
    count = lax.axis_size(axis)
    leading, last = (max(0, -steps), min(count, count - steps))
    return lax.ppermute(value, axis, [(source, source + steps) for source in range(leading, last)])


def combine(former, latter):
    return (former[0] * latter[0], latter[0] * former[1] + latter[1])


def recurrence(conv_rows, gate_pre_x, gate_pre_a, bias_pair, rates, places):
    group = conv_rows.shape[0]
    tokens = conv_rows.shape[1]
    width = conv_rows.shape[2]
    blocks = tokens // 8
    seq_total = lax.axis_size("seq") * tokens
    gate_x = jax.nn.sigmoid(gate_pre_x + bias_pair[0])
    gate_a = jax.nn.sigmoid(gate_pre_a + bias_pair[1])
    log_a = -8.0 * gate_a * rates / seq_total
    reset = (places == 0)[:, :, None]
    decay = jnp.where(reset, jnp.float32(0.0), jnp.exp(log_a))
    scale = jnp.where(reset, jnp.float32(1.0), jnp.sqrt(-jnp.expm1(2.0 * log_a)))
    drive = conv_rows.astype(jnp.float32) * gate_x * scale
    decay_blocks = decay.reshape(group, blocks, 8, width)
    drive_blocks = drive.reshape(group, blocks, 8, width)
    running_prod = jnp.ones((group, blocks, width), jnp.float32)
    running_state = jnp.zeros((group, blocks, width), jnp.float32)
    prod_list = []
    state_list = []
    for inner in range(8):
        step_decay = decay_blocks[:, :, inner, :]
        running_prod = running_prod * step_decay
        running_state = step_decay * running_state + drive_blocks[:, :, inner, :]
        prod_list.append(running_prod)
        state_list.append(running_state)
    block_prod = jnp.swapaxes(running_prod, 0, 1)
    block_state = jnp.swapaxes(running_state, 0, 1)

    def across(carry, pair):
        after = combine(carry, pair)
        return (after, carry)

    start = (jnp.ones((group, width), jnp.float32), jnp.zeros((group, width), jnp.float32))
    ending, befores = lax.scan(across, start, (block_prod, block_state))
    identity = (jnp.ones_like(ending[0]), jnp.zeros_like(ending[1]))
    incoming = prefix(ending, "seq", combine, identity)
    entering = befores[1] + befores[0] * incoming[1][None, :, :]
    entering = jnp.swapaxes(entering, 0, 1)[:, :, None, :]
    products = jnp.stack(prod_list, axis=2)
    local_state = jnp.stack(state_list, axis=2)
    full = local_state + products * entering
    return full.reshape(group, tokens, width).astype(jnp.bfloat16)


def general(
    branch_x, positions, teacher_held, gate_weights, gate_bias, conv_weight, conv_bias, decay_rate
):
    tokens = branch_x.shape[1]
    width = branch_x.shape[2]
    target = from_partner(teacher_held, "segment", 0)
    previous = from_behind(branch_x[:, -3:, :], "seq", 1)
    extended = jnp.concatenate([previous, branch_x], axis=1).astype(jnp.float32)
    conv = jnp.zeros((1, tokens, width), jnp.float32) + conv_bias
    for lag_steps in range(4):
        valid = (positions >= lag_steps).astype(jnp.float32)[:, :, None]
        conv = (
            conv
            + conv_weight[lag_steps]
            * extended[:, 3 - lag_steps : 3 - lag_steps + tokens, :]
            * valid
        )
    conv_rounded = conv.astype(jnp.bfloat16)
    by_heads = conv_rounded.reshape(1, tokens, HEADS, HS)
    preact = jnp.einsum(
        "nthi,hgij->ngthj",
        by_heads,
        lax.all_gather(gate_weights, "fsdp", axis=0, tiled=True),
        preferred_element_type=jnp.float32,
    )
    student = recurrence(
        conv_rounded,
        preact[:, 0].reshape(1, tokens, width),
        preact[:, 1].reshape(1, tokens, width),
        gate_bias,
        decay_rate,
        positions,
    )
    student_f = student.astype(jnp.float32)
    normed = student_f * lax.rsqrt(jnp.mean(student_f * student_f, axis=-1, keepdims=True) + 1e-06)
    token_loss = jnp.mean((normed - target.astype(jnp.float32)) ** 2, axis=-1)
    return (student, token_loss)


def in_vmem(count):
    return [pl.BlockSpec(memory_space=pltpu.VMEM)] * count


def pallas(kernel, name, out_shape, in_specs, out_specs, scratch_shapes, work, **more):
    return pl.pallas_call(
        kernel,
        out_shape=out_shape,
        in_specs=in_specs,
        out_specs=out_specs,
        scratch_shapes=scratch_shapes,
        compiler_params=pltpu.CompilerParams(vmem_limit_bytes=24 << 20),
        cost_estimate=pl.CostEstimate(
            flops=0, bytes_accessed=0, transcendentals=0
        ),
        name=name,
        **more,
    )


def cut_kernel(x_ref, w_ref, half_ref, quarter_ref, edge_ref, sem):
    here = lax.axis_index("seq")
    tokens = x_ref.shape[1]
    halves, quarters = half_ref.shape[0], quarter_ref.shape[0]
    copies = [
        pltpu.make_async_copy(
            w_ref.at[pl.ds(lax.rem(here, 2) * halves, halves)], half_ref, sem.at[0]
        ),
        pltpu.make_async_copy(w_ref.at[pl.ds(here * quarters, quarters)], quarter_ref, sem.at[1]),
        pltpu.make_async_copy(x_ref.at[0, pl.ds(tokens - EDGE, EDGE), :], edge_ref, sem.at[2]),
    ]
    for copy in copies:
        copy.start()
    for copy in copies:
        copy.wait()


def cut(branch_x, gate_weights):
    held = gate_weights.shape[0]
    rest = gate_weights.shape[1:]
    return pallas(
        cut_kernel,
        "cut",
        [
            jax.ShapeDtypeStruct((held // 2,) + rest, jnp.bfloat16),
            jax.ShapeDtypeStruct((held // 4,) + rest, jnp.bfloat16),
            jax.ShapeDtypeStruct((EDGE, branch_x.shape[2]), jnp.bfloat16),
        ],
        [pl.BlockSpec(memory_space=pltpu.HBM)] * 2,
        [pl.BlockSpec(memory_space=pl.ANY)] * 3,
        [pltpu.SemaphoreType.DMA((3,))],
        10000,
    )(
        pltpu.with_memory_space_constraint(branch_x, pltpu.HBM),
        pltpu.with_memory_space_constraint(gate_weights, pltpu.HBM),
    )


def spread(codes):
    tokens = codes.shape[1]
    down = lax.broadcasted_iota(jnp.int32, (tokens, tokens), 0)
    across = lax.broadcasted_iota(jnp.int32, (tokens, tokens), 1)
    diagonal = jnp.where(down == across, jnp.broadcast_to(codes, (tokens, tokens)), 0.0)
    return jnp.dot(
        diagonal.astype(jnp.bfloat16),
        jnp.ones((tokens, HS), jnp.bfloat16),
        preferred_element_type=jnp.float32,
    )


def lanes_of(head):
    return pl.ds(pl.multiple_of(head * HS, HS), HS)


def conv_kernel(x_ref, edge_ref, pos_ref, w_ref, b_ref, out_ref, mask_ref, rows, natural, lags):
    tokens = x_ref.shape[1]
    span = tokens // 8
    natural[...] = spread(jnp.minimum(pos_ref[...], 3).astype(jnp.float32))
    for step in range(span):
        code = natural[pl.ds(step, 8, stride=span), :]
        at = pl.ds(step * 8, 8)
        first = jnp.minimum(code, 1.0)
        mask_ref[0, at, :] = first
        mask_ref[1, at, :] = jnp.maximum(1.0 - first, 1e-37)
        lags[0, at, :] = jnp.clip(code - 1.0, 0.0, 1.0)
        lags[1, at, :] = jnp.clip(code - 2.0, 0.0, 1.0)

    def body(head, unused):
        lanes = lanes_of(head)
        rows[head, pl.ds(0, 8), :] = edge_ref[:, lanes].astype(jnp.float32)[EDGE - 8 :]
        rows[head, pl.ds(8, tokens), :] = x_ref[0, :, lanes].astype(jnp.float32)
        tiles = [rows[head, pl.ds(8 + step, 8, stride=span), :] for step in range(-3, span)]
        half = jnp.concatenate(tiles[3:], axis=0) * (w_ref[0:1, lanes] * 0.5) + (
            b_ref[0:1, lanes] * 0.5
        )
        for lag in range(1, 4):
            shifted = jnp.concatenate(tiles[3 - lag : 3 - lag + span], axis=0)
            mask = mask_ref[0] if lag == 1 else lags[lag - 2]
            half = half + shifted * (w_ref[lag : lag + 1, lanes] * 0.5) * mask
        out_ref[head] = half.astype(jnp.bfloat16)
        return unused

    lax.fori_loop(0, out_ref.shape[0], body, 0, unroll=4)


def conv_rows(branch_x, edge, positions, weight, bias):
    tokens, width = branch_x.shape[1:]
    heads = width // HS
    return pallas(
        conv_kernel,
        "conv_rows",
        [
            jax.ShapeDtypeStruct((heads, tokens, HS), jnp.bfloat16),
            jax.ShapeDtypeStruct((2, tokens, HS), jnp.float32),
        ],
        in_vmem(5),
        in_vmem(2),
        [
            pltpu.VMEM((heads, tokens + 8, HS), jnp.float32),
            pltpu.VMEM((tokens, HS), jnp.float32),
            pltpu.VMEM((2, tokens, HS), jnp.float32),
        ],
        tokens * width,
    )(branch_x, edge, positions, weight, bias)


def across_spans(product, state):
    place = lax.broadcasted_iota(jnp.int32, product.shape, 0)
    for apart in (1, 2, 4):
        reached = place >= apart
        before_p = jnp.where(reached, pltpu.roll(product, apart, 0), 1.0)
        before_s = jnp.where(reached, pltpu.roll(state, apart, 0), 0.0)
        state = product * before_s + state
        product = product * before_p
    enter_p = jnp.where(place >= 1, pltpu.roll(product, 1, 0), 1.0)
    enter_s = jnp.where(place >= 1, pltpu.roll(state, 1, 0), 0.0)
    return product, state, enter_p, enter_s


def gated(total, rounded, weights, masks, bias_ref, rate_ref, head, state_ref, prod_ref, place):
    lanes = lanes_of(head)
    span = rounded.shape[0] // 8
    pre = jnp.dot(rounded, weights, preferred_element_type=jnp.float32)
    gate_x = 1.0 + jnp.tanh(pre[:, :HS] + bias_ref[0:1, lanes] * 0.5)
    gate_a = 1.0 + jnp.tanh(pre[:, HS:] + bias_ref[1:2, lanes] * 0.5)
    power = gate_a * (rate_ref[0:1, lanes] * (-4.0 * LOG2E / total))
    decay = jnp.exp2(power)
    lost = jnp.tanh(power * -LN2)
    square = jnp.maximum(lost + lost * decay * decay, masks[1])
    drive = rounded.astype(jnp.float32) * gate_x * (square * lax.rsqrt(square))
    decay = decay * masks[0]
    product, state = jnp.ones((8, HS), jnp.float32), jnp.zeros((8, HS), jnp.float32)
    for step in range(span):
        at = slice(step * 8, step * 8 + 8)
        state = decay[at] * state + drive[at]
        product = product * decay[at]
        state_ref[place, at, :] = state
        prod_ref[place, at, :] = product
    return across_spans(product, state)


def shard_kernel(total, pair, counts, conv_ref, mask_ref, bias_ref, rate_ref, *refs):
    weights, refs = refs[: len(counts)], refs[len(counts) :]
    before, (state_ref, prod_ref, enter_ref, end_ref) = refs[:-4], refs[-4:]
    heads = state_ref.shape[0]
    row = 2 * heads * len(before)
    for slot, ref in enumerate(before):
        end_ref[pl.ds(2 * heads * slot, 2 * heads), :] = ref[...]
    base = lax.bitwise_xor(lax.axis_index("fsdp"), pair) * heads
    here = lax.axis_index("seq") if len(counts) == 4 else lax.rem(lax.axis_index("seq"), 2)
    masks = (mask_ref[0], mask_ref[1])
    for apart, (count, ref) in enumerate(zip(counts, weights)):
        first = lax.bitwise_xor(here, apart) * count if len(counts) > 1 else 0
        for index in range(count):
            place = first + index
            product, state, enter_p, enter_s = gated(
                total,
                conv_ref[base + place],
                jnp.concatenate([ref[index, 0], ref[index, 1]], axis=1),
                masks,
                bias_ref,
                rate_ref,
                base + place,
                state_ref,
                prod_ref,
                place,
            )
            enter_ref[place, 0] = enter_p
            enter_ref[place, 1] = enter_s
            end_ref[pl.ds(row + place, 1), :] = product[7:8]
            end_ref[pl.ds(row + heads + place, 1), :] = state[7:8]


def shard(conv, masks, params, pair, weights, total, before=()):
    tokens = conv.shape[1]
    counts = tuple(part.shape[0] for part in weights)
    heads = sum(counts)
    return pallas(
        functools.partial(shard_kernel, total, pair, counts),
        "shard",
        [
            jax.ShapeDtypeStruct((heads, tokens, HS), jnp.float32),
            jax.ShapeDtypeStruct((heads, tokens, HS), jnp.float32),
            jax.ShapeDtypeStruct((heads, 2, 8, HS), jnp.float32),
            jax.ShapeDtypeStruct((2 * heads * (1 + len(before)), HS), jnp.float32),
        ],
        in_vmem(4 + len(weights) + len(before)),
        in_vmem(4),
        [],
        heads * tokens * HS,
    )(conv, masks, *params, *weights, *before)


def natural_order(tokens):
    span = tokens // 8
    token = lax.broadcasted_iota(jnp.int32, (tokens, tokens), 0)
    row = lax.broadcasted_iota(jnp.int32, (tokens, tokens), 1)
    here = row == lax.rem(token, span) * 8 + lax.div(token, span)
    return jnp.where(here, 1.0, 0.0).astype(jnp.bfloat16)


def final_kernel(pairs, target_ref, *refs):
    devices = lax.axis_size("seq")
    here = lax.axis_index("seq")
    ends, refs = refs[: devices - 1], refs[devices - 1 :]
    parts = [refs[3 * slot : 3 * slot + 3] for slot in range(len(pairs))]
    student_ref, loss_ref, ends_s, held, sem = refs[3 * len(pairs) :]
    heads, tokens = parts[0][0].shape[:2]
    span = tokens // 8
    width = heads * HS
    for apart in range(1, devices):
        ends_s[lax.bitwise_xor(here, apart)] = ends[apart - 1][...]
    squares = jnp.zeros((tokens, HS), jnp.float32)
    copies = []
    bases = []
    order = natural_order(tokens)
    for slot, (pair, (state_ref, prod_ref, enter_ref)) in enumerate(zip(pairs, parts)):
        incoming = jnp.zeros((heads, HS), jnp.float32)
        row = 2 * heads * slot
        for place in range(devices - 1):
            after = ends_s[place, row : row + heads, :] * incoming + (
                ends_s[place, row + heads : row + 2 * heads, :]
            )
            incoming = jnp.where(place < here, after, incoming)
        base = lax.bitwise_xor(lax.axis_index("fsdp"), pair) * heads
        bases.append(base)
        for head in range(heads):
            at_head = slot * heads + head
            entering = enter_ref[head, 1] + enter_ref[head, 0] * incoming[head : head + 1]
            rows = [
                state_ref[head, step * 8 : step * 8 + 8, :]
                + prod_ref[head, step * 8 : step * 8 + 8, :] * entering
                for step in range(span)
            ]
            strided = jnp.concatenate(rows, axis=0).astype(jnp.bfloat16)
            value = jnp.dot(order, strided, preferred_element_type=jnp.float32)
            held[:, at_head * HS : (at_head + 1) * HS] = value.astype(jnp.bfloat16)
            squares = squares + value * value
        columns = pl.ds(pl.multiple_of(base * HS, width), width)
        copies.append(
            pltpu.make_async_copy(
                held.at[:, pl.ds(slot * width, width)], student_ref.at[0, :, columns], sem.at[slot]
            )
        )
        copies[-1].start()
    full = student_ref.shape[2]
    mean = jnp.sum(squares, axis=1, keepdims=True) * (1.0 / full)
    scale = jnp.broadcast_to(lax.rsqrt(mean + 1e-06), (tokens, HS))
    total = jnp.zeros((tokens, HS), jnp.float32)
    for slot, base in enumerate(bases):
        for head in range(heads):
            at_head = slot * heads + head
            value = held[:, at_head * HS : (at_head + 1) * HS].astype(jnp.float32)
            off = value * scale - target_ref[0, :, lanes_of(base + head)].astype(jnp.float32)
            total = total + off * off
    loss_ref[...] = jnp.sum(total.T, axis=0, keepdims=True) * (1.0 / full)
    for copy in copies:
        copy.wait()


def final(pairs, target, ends, parts):
    heads, tokens = parts[0][0].shape[:2]
    full = HEADS * HS
    flat = [array for part in parts for array in part[:3]]
    return pallas(
        functools.partial(final_kernel, pairs),
        "final",
        [
            jax.ShapeDtypeStruct((1, tokens, full), jnp.bfloat16),
            jax.ShapeDtypeStruct((1, tokens), jnp.float32),
        ],
        in_vmem(1 + len(ends) + len(flat)),
        [pl.BlockSpec(memory_space=pltpu.HBM)] + in_vmem(1),
        [
            pltpu.VMEM((len(ends) + 1,) + ends[0].shape, jnp.float32),
            pltpu.VMEM((tokens, full), jnp.bfloat16),
            pltpu.SemaphoreType.DMA((len(pairs),)),
        ],
        tokens * full,
    )(target, *ends, *flat)


def swap(value, axis, apart):
    return lax.ppermute(value, axis, [(i, i ^ apart) for i in range(lax.axis_size(axis))])


def after(value, *earlier):
    return lax.optimization_barrier((value, *earlier))[0]


def local(
    branch_x, positions, teacher_held, gate_weights, gate_bias, conv_weight, conv_bias, decay_rate
):
    tokens, width = branch_x.shape[1:]
    total = lax.axis_size("seq") * tokens
    half, quarter, edge = cut(branch_x, gate_weights)
    target = swap(teacher_held, "segment", 1)
    quarters = {pair: swap(quarter, "fsdp", pair) for pair in (2, 3)}
    half = swap(half, "fsdp", 1)
    edge = from_behind(edge, "seq", 1)
    conv, masks = conv_rows(branch_x, edge, positions, conv_weight, conv_bias.reshape(1, width))
    params = (gate_bias, decay_rate.reshape(1, width))
    parts = [shard(conv, masks, params, 0, [gate_weights], total)]
    two = swap(quarters[2], "seq", 2)
    three = swap(after(quarters[3], masks), "seq", 2)
    mine = after(quarters[2], two, parts[0][3])
    weights = [mine, swap(mine, "seq", 1), two, swap(two, "seq", 1)]
    parts.append(shard(conv, masks, params, 2, weights, total))
    half = after(half, two)
    weights = [half, swap(half, "seq", 1)]
    before = [part[3] for part in parts]
    parts.append(shard(conv, masks, params, 1, weights, total, ()))
    mine = after(quarters[3], three)
    weights = [mine, swap(mine, "seq", 1), three, swap(three, "seq", 1)]
    before = [part[3] for part in parts]
    parts.append(shard(conv, masks, params, 3, weights, total, before))
    end = parts[-1][3]
    ends = [swap(end, "seq", apart) for apart in (1, 2, 3)]
    return final((0, 2, 1, 3), target, ends, parts)


def solution(mesh):
    shards, devices = mesh.shape["fsdp"], mesh.shape["seq"]
    whole = shards == 4 and devices == 4
    in_specs = (
        P(("segment", "fsdp"), "seq", None),
        P(("segment", "fsdp"), "seq"),
        P(("segment", "fsdp"), "seq", None),
        P("fsdp", None, None, None),
        P(),
        P(),
        P(),
        P(),
    )
    out_specs = (P(("segment", "fsdp"), "seq", None), P(("segment", "fsdp"), "seq"))
    return jax.shard_map(
        local if whole else general,
        mesh=mesh,
        in_specs=in_specs,
        out_specs=out_specs,
        check_vma=False,
    )
```

```python
import functools
import math

import jax
import jax.numpy as jnp
from jax import lax
from jax.experimental import pallas as pl
from jax.experimental.pallas import tpu as pltpu
from jax.sharding import PartitionSpec as P

HEADS = 32
HS = 128
LOG2E = math.log2(math.e)
LN2 = math.log(2.0)
EDGE = 16


def prefix(value, axis, combine, identity):
    devices, here = (lax.axis_size(axis), lax.axis_index(axis))
    everything = jax.tree.map(lambda part: lax.all_gather(part, axis), value)
    start = jax.tree.map(
        lambda part, zero: jnp.broadcast_to(jnp.asarray(zero, part.dtype), part.shape),
        value,
        identity,
    )

    def hop(k, before):
        reached = k < here
        new = combine(before, jax.tree.map(lambda part: part[k], everything))
        return jax.tree.map(lambda a, b: jnp.where(reached, a, b), new, before)

    return lax.fori_loop(0, devices, hop, start)


def from_partner(value, axis, apart):
    return lax.ppermute(value, axis, [(i, i ^ 1 << apart) for i in range(lax.axis_size(axis))])


def from_behind(value, axis, steps):
    count = lax.axis_size(axis)
    leading, last = (max(0, -steps), min(count, count - steps))
    return lax.ppermute(value, axis, [(source, source + steps) for source in range(leading, last)])


def combine(former, latter):
    return (former[0] * latter[0], latter[0] * former[1] + latter[1])


def recurrence(conv_rows, gate_pre_x, gate_pre_a, bias_pair, rates, places):
    group = conv_rows.shape[0]
    tokens = conv_rows.shape[1]
    width = conv_rows.shape[2]
    blocks = tokens // 8
    seq_total = lax.axis_size("seq") * tokens
    gate_x = jax.nn.sigmoid(gate_pre_x + bias_pair[0])
    gate_a = jax.nn.sigmoid(gate_pre_a + bias_pair[1])
    log_a = -8.0 * gate_a * rates / seq_total
    reset = (places == 0)[:, :, None]
    decay = jnp.where(reset, jnp.float32(0.0), jnp.exp(log_a))
    scale = jnp.where(reset, jnp.float32(1.0), jnp.sqrt(-jnp.expm1(2.0 * log_a)))
    drive = conv_rows.astype(jnp.float32) * gate_x * scale
    decay_blocks = decay.reshape(group, blocks, 8, width)
    drive_blocks = drive.reshape(group, blocks, 8, width)
    running_prod = jnp.ones((group, blocks, width), jnp.float32)
    running_state = jnp.zeros((group, blocks, width), jnp.float32)
    prod_list = []
    state_list = []
    for inner in range(8):
        step_decay = decay_blocks[:, :, inner, :]
        running_prod = running_prod * step_decay
        running_state = step_decay * running_state + drive_blocks[:, :, inner, :]
        prod_list.append(running_prod)
        state_list.append(running_state)
    block_prod = jnp.swapaxes(running_prod, 0, 1)
    block_state = jnp.swapaxes(running_state, 0, 1)

    def across(carry, pair):
        after = combine(carry, pair)
        return (after, carry)

    start = (jnp.ones((group, width), jnp.float32), jnp.zeros((group, width), jnp.float32))
    ending, befores = lax.scan(across, start, (block_prod, block_state))
    identity = (jnp.ones_like(ending[0]), jnp.zeros_like(ending[1]))
    incoming = prefix(ending, "seq", combine, identity)
    entering = befores[1] + befores[0] * incoming[1][None, :, :]
    entering = jnp.swapaxes(entering, 0, 1)[:, :, None, :]
    products = jnp.stack(prod_list, axis=2)
    local_state = jnp.stack(state_list, axis=2)
    full = local_state + products * entering
    return full.reshape(group, tokens, width).astype(jnp.bfloat16)


def general(
    branch_x, positions, teacher_held, gate_weights, gate_bias, conv_weight, conv_bias, decay_rate
):
    tokens = branch_x.shape[1]
    width = branch_x.shape[2]
    target = from_partner(teacher_held, "segment", 0)
    previous = from_behind(branch_x[:, -3:, :], "seq", 1)
    extended = jnp.concatenate([previous, branch_x], axis=1).astype(jnp.float32)
    conv = jnp.zeros((1, tokens, width), jnp.float32) + conv_bias
    for lag_steps in range(4):
        valid = (positions >= lag_steps).astype(jnp.float32)[:, :, None]
        conv = (
            conv
            + conv_weight[lag_steps]
            * extended[:, 3 - lag_steps : 3 - lag_steps + tokens, :]
            * valid
        )
    conv_rounded = conv.astype(jnp.bfloat16)
    by_heads = conv_rounded.reshape(1, tokens, HEADS, HS)
    preact = jnp.einsum(
        "nthi,hgij->ngthj",
        by_heads,
        lax.all_gather(gate_weights, "fsdp", axis=0, tiled=True),
        preferred_element_type=jnp.float32,
    )
    student = recurrence(
        conv_rounded,
        preact[:, 0].reshape(1, tokens, width),
        preact[:, 1].reshape(1, tokens, width),
        gate_bias,
        decay_rate,
        positions,
    )
    student_f = student.astype(jnp.float32)
    normed = student_f * lax.rsqrt(jnp.mean(student_f * student_f, axis=-1, keepdims=True) + 1e-06)
    token_loss = jnp.mean((normed - target.astype(jnp.float32)) ** 2, axis=-1)
    return (student, token_loss)


def in_vmem(count):
    return [pl.BlockSpec(memory_space=pltpu.VMEM)] * count


def pallas(kernel, name, out_shape, in_specs, out_specs, scratch_shapes, weight=0, **more):
    return pl.pallas_call(
        kernel,
        out_shape=out_shape,
        in_specs=in_specs,
        out_specs=out_specs,
        scratch_shapes=scratch_shapes,
        compiler_params=pltpu.CompilerParams(vmem_limit_bytes=24 << 20),
        cost_estimate=pl.CostEstimate(
            flops=weight, bytes_accessed=0, transcendentals=0
        ),
        name=name,
        **more,
    )


def cut_kernel(x_ref, w_ref, half_ref, quarter_ref, edge_ref, sem):
    here = lax.axis_index("seq")
    tokens = x_ref.shape[1]
    halves, quarters = half_ref.shape[0], quarter_ref.shape[0]
    copies = [
        pltpu.make_async_copy(
            w_ref.at[pl.ds(lax.rem(here, 2) * halves, halves)], half_ref, sem.at[0]
        ),
        pltpu.make_async_copy(w_ref.at[pl.ds(here * quarters, quarters)], quarter_ref, sem.at[1]),
        pltpu.make_async_copy(x_ref.at[0, pl.ds(tokens - EDGE, EDGE), :], edge_ref, sem.at[2]),
    ]
    for copy in copies:
        copy.start()
    for copy in copies:
        copy.wait()


def cut(branch_x, gate_weights):
    held = gate_weights.shape[0]
    rest = gate_weights.shape[1:]
    return pallas(
        cut_kernel,
        "cut",
        [
            jax.ShapeDtypeStruct((held // 2,) + rest, jnp.bfloat16),
            jax.ShapeDtypeStruct((held // 4,) + rest, jnp.bfloat16),
            jax.ShapeDtypeStruct((EDGE, branch_x.shape[2]), jnp.bfloat16),
        ],
        [pl.BlockSpec(memory_space=pltpu.HBM)] * 2,
        [pl.BlockSpec(memory_space=pl.ANY)] * 3,
        [pltpu.SemaphoreType.DMA((3,))],
    )(
        pltpu.with_memory_space_constraint(branch_x, pltpu.HBM),
        pltpu.with_memory_space_constraint(gate_weights, pltpu.HBM),
    )


def spread(codes):
    tokens = codes.shape[1]
    down = lax.broadcasted_iota(jnp.int32, (tokens, tokens), 0)
    across = lax.broadcasted_iota(jnp.int32, (tokens, tokens), 1)
    diagonal = jnp.where(down == across, jnp.broadcast_to(codes, (tokens, tokens)), 0.0)
    return jnp.dot(
        diagonal.astype(jnp.bfloat16),
        jnp.ones((tokens, HS), jnp.bfloat16),
        preferred_element_type=jnp.float32,
    )


def lanes_of(head):
    return pl.ds(pl.multiple_of(head * HS, HS), HS)


def conv_kernel(x_ref, edge_ref, pos_ref, w_ref, b_ref, out_ref, mask_ref, rows, natural, lags):
    tokens = x_ref.shape[1]
    span = tokens // 8
    natural[...] = spread(jnp.minimum(pos_ref[...], 3).astype(jnp.float32))
    for step in range(span):
        code = natural[pl.ds(step, 8, stride=span), :]
        at = pl.ds(step * 8, 8)
        first = jnp.minimum(code, 1.0)
        mask_ref[0, at, :] = first
        mask_ref[1, at, :] = jnp.maximum(1.0 - first, 1e-37)
        lags[0, at, :] = jnp.clip(code - 1.0, 0.0, 1.0)
        lags[1, at, :] = jnp.clip(code - 2.0, 0.0, 1.0)

    def body(head, unused):
        lanes = lanes_of(head)
        rows[head, pl.ds(0, 8), :] = edge_ref[:, lanes].astype(jnp.float32)[EDGE - 8 :]
        rows[head, pl.ds(8, tokens), :] = x_ref[0, :, lanes].astype(jnp.float32)
        tiles = [rows[head, pl.ds(8 + step, 8, stride=span), :] for step in range(-3, span)]
        half = jnp.concatenate(tiles[3:], axis=0) * (w_ref[0:1, lanes] * 0.5) + (
            b_ref[0:1, lanes] * 0.5
        )
        for lag in range(1, 4):
            shifted = jnp.concatenate(tiles[3 - lag : 3 - lag + span], axis=0)
            mask = mask_ref[0] if lag == 1 else lags[lag - 2]
            half = half + shifted * (w_ref[lag : lag + 1, lanes] * 0.5) * mask
        out_ref[head] = half.astype(jnp.bfloat16)
        return unused

    lax.fori_loop(0, out_ref.shape[0], body, 0, unroll=4)


def conv_rows(branch_x, edge, positions, weight, bias):
    tokens, width = branch_x.shape[1:]
    heads = width // HS
    return pallas(
        conv_kernel,
        "conv_rows",
        [
            jax.ShapeDtypeStruct((heads, tokens, HS), jnp.bfloat16),
            jax.ShapeDtypeStruct((2, tokens, HS), jnp.float32),
        ],
        in_vmem(5),
        in_vmem(2),
        [
            pltpu.VMEM((heads, tokens + 8, HS), jnp.float32),
            pltpu.VMEM((tokens, HS), jnp.float32),
            pltpu.VMEM((2, tokens, HS), jnp.float32),
        ],
    )(branch_x, edge, positions, weight, bias)


def across_spans(product, state):
    place = lax.broadcasted_iota(jnp.int32, product.shape, 0)
    for apart in (1, 2, 4):
        reached = place >= apart
        before_p = jnp.where(reached, pltpu.roll(product, apart, 0), 1.0)
        before_s = jnp.where(reached, pltpu.roll(state, apart, 0), 0.0)
        state = product * before_s + state
        product = product * before_p
    enter_p = jnp.where(place >= 1, pltpu.roll(product, 1, 0), 1.0)
    enter_s = jnp.where(place >= 1, pltpu.roll(state, 1, 0), 0.0)
    return product, state, enter_p, enter_s


def gated(total, rounded, weights, masks, bias_ref, rate_ref, head, state_ref, prod_ref, place):
    lanes = lanes_of(head)
    span = rounded.shape[0] // 8
    pre = jnp.dot(rounded, weights, preferred_element_type=jnp.float32)
    gate_x = 1.0 + jnp.tanh(pre[:, :HS] + bias_ref[0:1, lanes] * 0.5)
    gate_a = 1.0 + jnp.tanh(pre[:, HS:] + bias_ref[1:2, lanes] * 0.5)
    power = gate_a * (rate_ref[0:1, lanes] * (-4.0 * LOG2E / total))
    decay = jnp.exp2(power)
    lost = jnp.tanh(power * -LN2)
    square = jnp.maximum(lost + lost * decay * decay, masks[1])
    drive = rounded.astype(jnp.float32) * gate_x * (square * lax.rsqrt(square))
    decay = decay * masks[0]
    product, state = jnp.ones((8, HS), jnp.float32), jnp.zeros((8, HS), jnp.float32)
    for step in range(span):
        at = slice(step * 8, step * 8 + 8)
        state = decay[at] * state + drive[at]
        product = product * decay[at]
        state_ref[place, at, :] = state
        prod_ref[place, at, :] = product
    return across_spans(product, state)


def shard_kernel(total, pair, counts, conv_ref, mask_ref, bias_ref, rate_ref, *refs):
    weights, refs = refs[: len(counts)], refs[len(counts) :]
    before, (state_ref, prod_ref, enter_ref, end_ref) = refs[:-4], refs[-4:]
    heads = state_ref.shape[0]
    row = 2 * heads * len(before)
    for slot, ref in enumerate(before):
        end_ref[pl.ds(2 * heads * slot, 2 * heads), :] = ref[...]
    base = lax.bitwise_xor(lax.axis_index("fsdp"), pair) * heads
    here = lax.axis_index("seq") if len(counts) == 4 else lax.rem(lax.axis_index("seq"), 2)
    masks = (mask_ref[0], mask_ref[1])
    for apart, (count, ref) in enumerate(zip(counts, weights)):
        first = lax.bitwise_xor(here, apart) * count if len(counts) > 1 else 0
        for index in range(count):
            place = first + index
            product, state, enter_p, enter_s = gated(
                total,
                conv_ref[base + place],
                jnp.concatenate([ref[index, 0], ref[index, 1]], axis=1),
                masks,
                bias_ref,
                rate_ref,
                base + place,
                state_ref,
                prod_ref,
                place,
            )
            enter_ref[place, 0] = enter_p
            enter_ref[place, 1] = enter_s
            end_ref[pl.ds(row + place, 1), :] = product[7:8]
            end_ref[pl.ds(row + heads + place, 1), :] = state[7:8]


def shard(conv, masks, params, pair, weights, total, before=()):
    tokens = conv.shape[1]
    counts = tuple(part.shape[0] for part in weights)
    heads = sum(counts)
    return pallas(
        functools.partial(shard_kernel, total, pair, counts),
        "shard",
        [
            jax.ShapeDtypeStruct((heads, tokens, HS), jnp.float32),
            jax.ShapeDtypeStruct((heads, tokens, HS), jnp.float32),
            jax.ShapeDtypeStruct((heads, 2, 8, HS), jnp.float32),
            jax.ShapeDtypeStruct((2 * heads * (1 + len(before)), HS), jnp.float32),
        ],
        in_vmem(4 + len(weights) + len(before)),
        in_vmem(4),
        [],
        5500000000 if before else 0,
    )(conv, masks, *params, *weights, *before)


def lay_kernel(*refs):
    state_out, prod_out = refs[-2:]
    parts = [refs[at : at + 3] for at in range(0, len(refs) - 2, 3)]
    heads, tokens = parts[0][0].shape[:2]
    span = tokens // 8
    for slot, (state_ref, prod_ref, enter_ref) in enumerate(parts):
        for head in range(heads):
            enter_p, enter_s = enter_ref[head, 0], enter_ref[head, 1]
            for step in range(span):
                at = slice(step * 8, step * 8 + 8)
                product = prod_ref[head, at, :]
                natural = pl.ds(step, 8, stride=span)
                state_out[slot * heads + head, natural, :] = state_ref[head, at, :] + product * enter_s
                prod_out[slot * heads + head, natural, :] = product * enter_p


def lay_out(parts):
    heads, tokens = parts[0][0].shape[:2]
    flat = [array for part in parts for array in part[:3]]
    whole = jax.ShapeDtypeStruct((len(parts) * heads, tokens, HS), jnp.float32)
    return pallas(
        lay_kernel,
        "lay_out",
        [whole, whole],
        in_vmem(len(flat)),
        in_vmem(2),
        [],
    )(*flat)


def final_kernel(pairs, target_ref, state_ref, prod_ref, *refs):
    devices = lax.axis_size("seq")
    here = lax.axis_index("seq")
    ends, (student_ref, loss_ref, ends_s, held, sem) = refs[: devices - 1], refs[devices - 1 :]
    tokens = state_ref.shape[1]
    heads = state_ref.shape[0] // len(pairs)
    width = heads * HS
    for apart in range(1, devices):
        ends_s[lax.bitwise_xor(here, apart)] = ends[apart - 1][...]
    squares = jnp.zeros((tokens, HS), jnp.float32)
    copies = []
    bases = []
    for slot, pair in enumerate(pairs):
        incoming = jnp.zeros((heads, HS), jnp.float32)
        row = 2 * heads * slot
        for place in range(devices - 1):
            after = ends_s[place, row : row + heads, :] * incoming + (
                ends_s[place, row + heads : row + 2 * heads, :]
            )
            incoming = jnp.where(place < here, after, incoming)
        base = lax.bitwise_xor(lax.axis_index("fsdp"), pair) * heads
        bases.append(base)
        for head in range(heads):
            at_head = slot * heads + head
            rounded = (
                state_ref[at_head] + prod_ref[at_head] * incoming[head : head + 1]
            ).astype(jnp.bfloat16)
            student_ref[0, :, lanes_of(base + head)] = rounded
            value = rounded.astype(jnp.float32)
            squares = squares + value * value
    full = student_ref.shape[2]
    mean = jnp.sum(squares, axis=1, keepdims=True) * (1.0 / full)
    scale = jnp.broadcast_to(lax.rsqrt(mean + 1e-06), (tokens, HS))
    total = jnp.zeros((tokens, HS), jnp.float32)
    for slot, base in enumerate(bases):
        for head in range(heads):
            at_head = slot * heads + head
            value = student_ref[0, :, lanes_of(base + head)].astype(jnp.float32)
            off = value * scale - target_ref[0, :, lanes_of(base + head)].astype(jnp.float32)
            total = total + off * off
    loss_ref[...] = jnp.sum(total.T, axis=0, keepdims=True) * (1.0 / full)
    for copy in copies:
        copy.wait()


def final(pairs, target, states, products, ends):
    tokens = states.shape[1]
    full = HEADS * HS
    return pallas(
        functools.partial(final_kernel, pairs),
        "final",
        [
            jax.ShapeDtypeStruct((1, tokens, full), jnp.bfloat16),
            jax.ShapeDtypeStruct((1, tokens), jnp.float32),
        ],
        in_vmem(3 + len(ends)),
        in_vmem(2),
        [
            pltpu.VMEM((len(ends) + 1,) + ends[0].shape, jnp.float32),
            pltpu.VMEM((tokens, full), jnp.bfloat16),
            pltpu.SemaphoreType.DMA((len(pairs),)),
        ],
    )(target, states, products, *ends)


def swap(value, axis, apart):
    return lax.ppermute(value, axis, [(i, i ^ apart) for i in range(lax.axis_size(axis))])


def after(value, *earlier):
    return lax.optimization_barrier((value, *earlier))[0]


def local(
    branch_x, positions, teacher_held, gate_weights, gate_bias, conv_weight, conv_bias, decay_rate
):
    tokens, width = branch_x.shape[1:]
    total = lax.axis_size("seq") * tokens
    target = swap(teacher_held, "segment", 1)
    half, quarter, edge = cut(branch_x, gate_weights)
    quarters = {pair: swap(quarter, "fsdp", pair) for pair in (2, 3)}
    half = swap(half, "fsdp", 1)
    edge = from_behind(edge, "seq", 1)
    conv, masks = conv_rows(branch_x, edge, positions, conv_weight, conv_bias.reshape(1, width))
    params = (gate_bias, decay_rate.reshape(1, width))
    parts = [shard(conv, masks, params, 0, [gate_weights], total)]
    two = swap(quarters[2], "seq", 2)
    three = swap(after(quarters[3], masks), "seq", 2)
    mine = after(quarters[2], two, parts[0][3])
    weights = [mine, swap(mine, "seq", 1), two, swap(two, "seq", 1)]
    parts.append(shard(conv, masks, params, 2, weights, total))
    half = after(half, two)
    weights = [half, swap(half, "seq", 1)]
    before = [part[3] for part in parts]
    parts.append(shard(conv, masks, params, 1, weights, total, ()))
    mine = after(quarters[3], three)
    weights = [mine, swap(mine, "seq", 1), three, swap(three, "seq", 1)]
    before = [part[3] for part in parts]
    parts.append(shard(conv, masks, params, 3, weights, total, before))
    end = parts[-1][3]
    ends = [swap(end, "seq", apart) for apart in (1, 2, 3)]
    states, products = lay_out(parts)
    return final((0, 2, 1, 3), target, states, products, ends)


def solution(mesh):
    shards, devices = mesh.shape["fsdp"], mesh.shape["seq"]
    whole = shards == 4 and devices == 4
    in_specs = (
        P(("segment", "fsdp"), "seq", None),
        P(("segment", "fsdp"), "seq"),
        P(("segment", "fsdp"), "seq", None),
        P("fsdp", None, None, None),
        P(),
        P(),
        P(),
        P(),
    )
    out_specs = (P(("segment", "fsdp"), "seq", None), P(("segment", "fsdp"), "seq"))
    return jax.shard_map(
        local if whole else general,
        mesh=mesh,
        in_specs=in_specs,
        out_specs=out_specs,
        check_vma=False,
    )
```

```python
import functools
import math

import jax
import jax.numpy as jnp
from jax import lax
from jax.experimental import pallas as pl
from jax.experimental.pallas import tpu as pltpu
from jax.sharding import PartitionSpec as P

HEADS = 32
HS = 128
LOG2E = math.log2(math.e)
LN2 = math.log(2.0)
EDGE = 16


def prefix(value, axis, combine, identity):
    devices, here = (lax.axis_size(axis), lax.axis_index(axis))
    everything = jax.tree.map(lambda part: lax.all_gather(part, axis), value)
    start = jax.tree.map(
        lambda part, zero: jnp.broadcast_to(jnp.asarray(zero, part.dtype), part.shape),
        value,
        identity,
    )

    def hop(k, before):
        reached = k < here
        new = combine(before, jax.tree.map(lambda part: part[k], everything))
        return jax.tree.map(lambda a, b: jnp.where(reached, a, b), new, before)

    return lax.fori_loop(0, devices, hop, start)


def from_partner(value, axis, apart):
    return lax.ppermute(value, axis, [(i, i ^ 1 << apart) for i in range(lax.axis_size(axis))])


def from_behind(value, axis, steps):
    count = lax.axis_size(axis)
    leading, last = (max(0, -steps), min(count, count - steps))
    return lax.ppermute(value, axis, [(source, source + steps) for source in range(leading, last)])


def combine(former, latter):
    return (former[0] * latter[0], latter[0] * former[1] + latter[1])


def recurrence(conv_rows, gate_pre_x, gate_pre_a, bias_pair, rates, places):
    group = conv_rows.shape[0]
    tokens = conv_rows.shape[1]
    width = conv_rows.shape[2]
    blocks = tokens // 8
    seq_total = lax.axis_size("seq") * tokens
    gate_x = jax.nn.sigmoid(gate_pre_x + bias_pair[0])
    gate_a = jax.nn.sigmoid(gate_pre_a + bias_pair[1])
    log_a = -8.0 * gate_a * rates / seq_total
    reset = (places == 0)[:, :, None]
    decay = jnp.where(reset, jnp.float32(0.0), jnp.exp(log_a))
    scale = jnp.where(reset, jnp.float32(1.0), jnp.sqrt(-jnp.expm1(2.0 * log_a)))
    drive = conv_rows.astype(jnp.float32) * gate_x * scale
    decay_blocks = decay.reshape(group, blocks, 8, width)
    drive_blocks = drive.reshape(group, blocks, 8, width)
    running_prod = jnp.ones((group, blocks, width), jnp.float32)
    running_state = jnp.zeros((group, blocks, width), jnp.float32)
    prod_list = []
    state_list = []
    for inner in range(8):
        step_decay = decay_blocks[:, :, inner, :]
        running_prod = running_prod * step_decay
        running_state = step_decay * running_state + drive_blocks[:, :, inner, :]
        prod_list.append(running_prod)
        state_list.append(running_state)
    block_prod = jnp.swapaxes(running_prod, 0, 1)
    block_state = jnp.swapaxes(running_state, 0, 1)

    def across(carry, pair):
        after = combine(carry, pair)
        return (after, carry)

    start = (jnp.ones((group, width), jnp.float32), jnp.zeros((group, width), jnp.float32))
    ending, befores = lax.scan(across, start, (block_prod, block_state))
    identity = (jnp.ones_like(ending[0]), jnp.zeros_like(ending[1]))
    incoming = prefix(ending, "seq", combine, identity)
    entering = befores[1] + befores[0] * incoming[1][None, :, :]
    entering = jnp.swapaxes(entering, 0, 1)[:, :, None, :]
    products = jnp.stack(prod_list, axis=2)
    local_state = jnp.stack(state_list, axis=2)
    full = local_state + products * entering
    return full.reshape(group, tokens, width).astype(jnp.bfloat16)


def general(
    branch_x, positions, teacher_held, gate_weights, gate_bias, conv_weight, conv_bias, decay_rate
):
    tokens = branch_x.shape[1]
    width = branch_x.shape[2]
    target = from_partner(teacher_held, "segment", 0)
    previous = from_behind(branch_x[:, -3:, :], "seq", 1)
    extended = jnp.concatenate([previous, branch_x], axis=1).astype(jnp.float32)
    conv = jnp.zeros((1, tokens, width), jnp.float32) + conv_bias
    for lag_steps in range(4):
        valid = (positions >= lag_steps).astype(jnp.float32)[:, :, None]
        conv = (
            conv
            + conv_weight[lag_steps]
            * extended[:, 3 - lag_steps : 3 - lag_steps + tokens, :]
            * valid
        )
    conv_rounded = conv.astype(jnp.bfloat16)
    by_heads = conv_rounded.reshape(1, tokens, HEADS, HS)
    preact = jnp.einsum(
        "nthi,hgij->ngthj",
        by_heads,
        lax.all_gather(gate_weights, "fsdp", axis=0, tiled=True),
        preferred_element_type=jnp.float32,
    )
    student = recurrence(
        conv_rounded,
        preact[:, 0].reshape(1, tokens, width),
        preact[:, 1].reshape(1, tokens, width),
        gate_bias,
        decay_rate,
        positions,
    )
    student_f = student.astype(jnp.float32)
    normed = student_f * lax.rsqrt(jnp.mean(student_f * student_f, axis=-1, keepdims=True) + 1e-06)
    token_loss = jnp.mean((normed - target.astype(jnp.float32)) ** 2, axis=-1)
    return (student, token_loss)


def in_vmem(count):
    return [pl.BlockSpec(memory_space=pltpu.VMEM)] * count


def pallas(kernel, name, out_shape, in_specs, out_specs, scratch_shapes, weight=0, **more):
    return pl.pallas_call(
        kernel,
        out_shape=out_shape,
        in_specs=in_specs,
        out_specs=out_specs,
        scratch_shapes=scratch_shapes,
        compiler_params=pltpu.CompilerParams(vmem_limit_bytes=24 << 20),
        cost_estimate=pl.CostEstimate(
            flops=weight, bytes_accessed=0, transcendentals=0
        ),
        name=name,
        **more,
    )


def cut_kernel(x_ref, w_ref, *refs):
    small, refs = refs[: len(refs) // 2 - 2], refs[len(refs) // 2 - 2 :]
    half_ref, quarter_ref, edge_ref, *near, sem = refs
    here = lax.axis_index("seq")
    tokens = x_ref.shape[1]
    halves, quarters = half_ref.shape[0], quarter_ref.shape[0]
    copies = [
        pltpu.make_async_copy(
            w_ref.at[pl.ds(lax.rem(here, 2) * halves, halves)], half_ref, sem.at[0]
        ),
        pltpu.make_async_copy(w_ref.at[pl.ds(here * quarters, quarters)], quarter_ref, sem.at[1]),
        pltpu.make_async_copy(x_ref.at[0, pl.ds(tokens - EDGE, EDGE), :], edge_ref, sem.at[2]),
    ]
    for index, (source, target) in enumerate(zip(small, near)):
        copies.append(pltpu.make_async_copy(source, target, sem.at[3 + index]))
    for copy in copies:
        copy.start()
    for copy in copies:
        copy.wait()


def cut(branch_x, gate_weights, *small):
    held = gate_weights.shape[0]
    rest = gate_weights.shape[1:]
    return pallas(
        cut_kernel,
        "cut",
        [
            jax.ShapeDtypeStruct((held // 2,) + rest, jnp.bfloat16),
            jax.ShapeDtypeStruct((held // 4,) + rest, jnp.bfloat16),
            jax.ShapeDtypeStruct((EDGE, branch_x.shape[2]), jnp.bfloat16),
        ]
        + [jax.ShapeDtypeStruct(value.shape, value.dtype) for value in small],
        [pl.BlockSpec(memory_space=pltpu.HBM)] * (2 + len(small)),
        [pl.BlockSpec(memory_space=pl.ANY)] * (3 + len(small)),
        [pltpu.SemaphoreType.DMA((3 + len(small),))],
    )(
        *[
            pltpu.with_memory_space_constraint(value, pltpu.HBM)
            for value in (branch_x, gate_weights, *small)
        ]
    )


def spread(codes):
    tokens = codes.shape[1]
    down = lax.broadcasted_iota(jnp.int32, (tokens, tokens), 0)
    across = lax.broadcasted_iota(jnp.int32, (tokens, tokens), 1)
    diagonal = jnp.where(down == across, jnp.broadcast_to(codes, (tokens, tokens)), 0.0)
    return jnp.dot(
        diagonal.astype(jnp.bfloat16),
        jnp.ones((tokens, HS), jnp.bfloat16),
        preferred_element_type=jnp.float32,
    )


def lanes_of(head):
    return pl.ds(pl.multiple_of(head * HS, HS), HS)


def conv_kernel(x_ref, edge_ref, pos_ref, w_ref, b_ref, out_ref, mask_ref, rows, natural, lags):
    tokens = x_ref.shape[1]
    span = tokens // 8
    natural[...] = spread(jnp.minimum(pos_ref[...], 3).astype(jnp.float32))
    for step in range(span):
        code = natural[pl.ds(step, 8, stride=span), :]
        at = pl.ds(step * 8, 8)
        first = jnp.minimum(code, 1.0)
        mask_ref[0, at, :] = first
        mask_ref[1, at, :] = jnp.maximum(1.0 - first, 1e-37)
        lags[0, at, :] = jnp.clip(code - 1.0, 0.0, 1.0)
        lags[1, at, :] = jnp.clip(code - 2.0, 0.0, 1.0)

    def body(head, unused):
        lanes = lanes_of(head)
        rows[head, pl.ds(0, 8), :] = edge_ref[:, lanes].astype(jnp.float32)[EDGE - 8 :]
        rows[head, pl.ds(8, tokens), :] = x_ref[0, :, lanes].astype(jnp.float32)
        tiles = [rows[head, pl.ds(8 + step, 8, stride=span), :] for step in range(-3, span)]
        half = jnp.concatenate(tiles[3:], axis=0) * (w_ref[0:1, lanes] * 0.5) + (
            b_ref[0:1, lanes] * 0.5
        )
        for lag in range(1, 4):
            shifted = jnp.concatenate(tiles[3 - lag : 3 - lag + span], axis=0)
            mask = mask_ref[0] if lag == 1 else lags[lag - 2]
            half = half + shifted * (w_ref[lag : lag + 1, lanes] * 0.5) * mask
        out_ref[head] = half.astype(jnp.bfloat16)
        return unused

    lax.fori_loop(0, out_ref.shape[0], body, 0, unroll=4)


def conv_rows(branch_x, edge, positions, weight, bias):
    tokens, width = branch_x.shape[1:]
    heads = width // HS
    return pallas(
        conv_kernel,
        "conv_rows",
        [
            jax.ShapeDtypeStruct((heads, tokens, HS), jnp.bfloat16),
            jax.ShapeDtypeStruct((2, tokens, HS), jnp.float32),
        ],
        in_vmem(5),
        in_vmem(2),
        [
            pltpu.VMEM((heads, tokens + 8, HS), jnp.float32),
            pltpu.VMEM((tokens, HS), jnp.float32),
            pltpu.VMEM((2, tokens, HS), jnp.float32),
        ],
    )(branch_x, edge, positions, weight, bias)


def across_spans(product, state):
    place = lax.broadcasted_iota(jnp.int32, product.shape, 0)
    for apart in (1, 2, 4):
        reached = place >= apart
        before_p = jnp.where(reached, pltpu.roll(product, apart, 0), 1.0)
        before_s = jnp.where(reached, pltpu.roll(state, apart, 0), 0.0)
        state = product * before_s + state
        product = product * before_p
    enter_p = jnp.where(place >= 1, pltpu.roll(product, 1, 0), 1.0)
    enter_s = jnp.where(place >= 1, pltpu.roll(state, 1, 0), 0.0)
    return product, state, enter_p, enter_s


def gated(total, rounded, weights, masks, bias_ref, rate_ref, head, state_ref, prod_ref, place):
    lanes = lanes_of(head)
    span = rounded.shape[0] // 8
    pre = jnp.dot(rounded, weights, preferred_element_type=jnp.float32)
    gate_x = 1.0 + jnp.tanh(pre[:, :HS] + bias_ref[0:1, lanes] * 0.5)
    gate_a = 1.0 + jnp.tanh(pre[:, HS:] + bias_ref[1:2, lanes] * 0.5)
    power = gate_a * (rate_ref[0:1, lanes] * (-4.0 * LOG2E / total))
    decay = jnp.exp2(power)
    lost = jnp.tanh(power * -LN2)
    square = jnp.maximum(lost + lost * decay * decay, masks[1])
    drive = rounded.astype(jnp.float32) * gate_x * (square * lax.rsqrt(square))
    decay = decay * masks[0]
    product, state = jnp.ones((8, HS), jnp.float32), jnp.zeros((8, HS), jnp.float32)
    for step in range(span):
        at = slice(step * 8, step * 8 + 8)
        state = decay[at] * state + drive[at]
        product = product * decay[at]
        state_ref[place, at, :] = state
        prod_ref[place, at, :] = product
    return across_spans(product, state)


def shard_kernel(total, pair, counts, conv_ref, mask_ref, bias_ref, rate_ref, *refs):
    weights, refs = refs[: len(counts)], refs[len(counts) :]
    before, (state_ref, prod_ref, enter_ref, end_ref) = refs[:-4], refs[-4:]
    heads = state_ref.shape[0]
    row = 2 * heads * len(before)
    for slot, ref in enumerate(before):
        end_ref[pl.ds(2 * heads * slot, 2 * heads), :] = ref[...]
    base = lax.bitwise_xor(lax.axis_index("fsdp"), pair) * heads
    here = lax.axis_index("seq") if len(counts) == 4 else lax.rem(lax.axis_index("seq"), 2)
    masks = (mask_ref[0], mask_ref[1])
    for apart, (count, ref) in enumerate(zip(counts, weights)):
        first = lax.bitwise_xor(here, apart) * count if len(counts) > 1 else 0
        for index in range(count):
            place = first + index
            product, state, enter_p, enter_s = gated(
                total,
                conv_ref[base + place],
                jnp.concatenate([ref[index, 0], ref[index, 1]], axis=1),
                masks,
                bias_ref,
                rate_ref,
                base + place,
                state_ref,
                prod_ref,
                place,
            )
            enter_ref[place, 0] = enter_p
            enter_ref[place, 1] = enter_s
            end_ref[pl.ds(row + place, 1), :] = product[7:8]
            end_ref[pl.ds(row + heads + place, 1), :] = state[7:8]


def shard(conv, masks, params, pair, weights, total, before=()):
    tokens = conv.shape[1]
    counts = tuple(part.shape[0] for part in weights)
    heads = sum(counts)
    return pallas(
        functools.partial(shard_kernel, total, pair, counts),
        "shard",
        [
            jax.ShapeDtypeStruct((heads, tokens, HS), jnp.float32),
            jax.ShapeDtypeStruct((heads, tokens, HS), jnp.float32),
            jax.ShapeDtypeStruct((heads, 2, 8, HS), jnp.float32),
            jax.ShapeDtypeStruct((2 * heads * (1 + len(before)), HS), jnp.float32),
        ],
        in_vmem(4 + len(weights) + len(before)),
        in_vmem(4),
        [],
        5500000000 if before else 0,
    )(conv, masks, *params, *weights, *before)


def lay_kernel(*refs):
    state_out, prod_out = refs[-2:]
    parts = [refs[at : at + 3] for at in range(0, len(refs) - 2, 3)]
    heads, tokens = parts[0][0].shape[:2]
    span = tokens // 8
    for slot, (state_ref, prod_ref, enter_ref) in enumerate(parts):
        for head in range(heads):
            enter_p, enter_s = enter_ref[head, 0], enter_ref[head, 1]
            for step in range(span):
                at = slice(step * 8, step * 8 + 8)
                product = prod_ref[head, at, :]
                natural = pl.ds(step, 8, stride=span)
                state_out[slot * heads + head, natural, :] = state_ref[head, at, :] + product * enter_s
                prod_out[slot * heads + head, natural, :] = product * enter_p


def lay_out(parts):
    heads, tokens = parts[0][0].shape[:2]
    flat = [array for part in parts for array in part[:3]]
    whole = jax.ShapeDtypeStruct((len(parts) * heads, tokens, HS), jnp.float32)
    return pallas(
        lay_kernel,
        "lay_out",
        [whole, whole],
        in_vmem(len(flat)),
        in_vmem(2),
        [],
    )(*flat)


def enter_kernel(pairs, state_ref, prod_ref, *refs):
    devices = lax.axis_size("seq")
    here = lax.axis_index("seq")
    ends, (rows_ref, scale_ref, ends_s) = refs[: devices - 1], refs[devices - 1 :]
    tokens, full = rows_ref.shape
    heads = state_ref.shape[0] // len(pairs)
    for apart in range(1, devices):
        ends_s[lax.bitwise_xor(here, apart)] = ends[apart - 1][...]
    squares = jnp.zeros((tokens, HS), jnp.float32)
    for slot, pair in enumerate(pairs):
        incoming = jnp.zeros((heads, HS), jnp.float32)
        row = 2 * heads * slot
        for place in range(devices - 1):
            after = ends_s[place, row : row + heads, :] * incoming + (
                ends_s[place, row + heads : row + 2 * heads, :]
            )
            incoming = jnp.where(place < here, after, incoming)
        base = lax.bitwise_xor(lax.axis_index("fsdp"), pair) * heads
        for head in range(heads):
            at_head = slot * heads + head
            rounded = (
                state_ref[at_head] + prod_ref[at_head] * incoming[head : head + 1]
            ).astype(jnp.bfloat16)
            rows_ref[:, lanes_of(base + head)] = rounded
            value = rounded.astype(jnp.float32)
            squares = squares + value * value
    mean = jnp.sum(squares, axis=1, keepdims=True) * (1.0 / full)
    scale_ref[...] = jnp.broadcast_to(lax.rsqrt(mean + 1e-06), (tokens, HS))


def enter(pairs, states, products, ends):
    tokens = states.shape[1]
    return pallas(
        functools.partial(enter_kernel, pairs),
        "enter",
        [
            jax.ShapeDtypeStruct((tokens, HEADS * HS), jnp.bfloat16),
            jax.ShapeDtypeStruct((tokens, HS), jnp.float32),
        ],
        in_vmem(2 + len(ends)),
        in_vmem(2),
        [pltpu.VMEM((len(ends) + 1,) + ends[0].shape, jnp.float32)],
    )(states, products, *ends)


def loss_kernel(rows_ref, scale_ref, target_ref, student_ref, loss_ref, sem):
    tokens, full = rows_ref.shape
    copy = pltpu.make_async_copy(rows_ref, student_ref.at[0], sem)
    copy.start()
    scale = scale_ref[...]
    total = jnp.zeros((tokens, HS), jnp.float32)
    for start in range(0, full, HS):
        lanes = slice(start, start + HS)
        off = rows_ref[:, lanes].astype(jnp.float32) * scale - target_ref[0, :, lanes].astype(
            jnp.float32
        )
        total = total + off * off
    loss_ref[...] = jnp.sum(total.T, axis=0, keepdims=True) * (1.0 / full)
    copy.wait()


def losses(rows, scale, target):
    tokens, full = rows.shape
    return pallas(
        loss_kernel,
        "losses",
        [
            jax.ShapeDtypeStruct((1, tokens, full), jnp.bfloat16),
            jax.ShapeDtypeStruct((1, tokens), jnp.float32),
        ],
        in_vmem(3),
        [pl.BlockSpec(memory_space=pltpu.HBM)] + in_vmem(1),
        [pltpu.SemaphoreType.DMA],
    )(rows, scale, target)


def swap(value, axis, apart):
    return lax.ppermute(value, axis, [(i, i ^ apart) for i in range(lax.axis_size(axis))])


def after(value, *earlier):
    return lax.optimization_barrier((value, *earlier))[0]


def local(
    branch_x, positions, teacher_held, gate_weights, gate_bias, conv_weight, conv_bias, decay_rate
):
    tokens, width = branch_x.shape[1:]
    total = lax.axis_size("seq") * tokens
    target = swap(teacher_held, "segment", 1)
    half, quarter, edge, *small = cut(
        branch_x, gate_weights, positions, conv_weight, conv_bias.reshape(1, width)
    )
    quarters = {pair: swap(quarter, "fsdp", pair) for pair in (2, 3)}
    half = swap(half, "fsdp", 1)
    edge = from_behind(edge, "seq", 1)
    conv, masks = conv_rows(branch_x, edge, *small)
    params = (gate_bias, decay_rate.reshape(1, width))
    parts = [shard(conv, masks, params, 0, [gate_weights], total)]
    two = swap(quarters[2], "seq", 2)
    three = swap(after(quarters[3], masks), "seq", 2)
    mine = after(quarters[2], two, parts[0][3])
    weights = [mine, swap(mine, "seq", 1), two, swap(two, "seq", 1)]
    parts.append(shard(conv, masks, params, 2, weights, total))
    half = after(half, two)
    weights = [half, swap(half, "seq", 1)]
    before = [part[3] for part in parts]
    parts.append(shard(conv, masks, params, 1, weights, total, ()))
    mine = after(quarters[3], three)
    weights = [mine, swap(mine, "seq", 1), three, swap(three, "seq", 1)]
    before = [part[3] for part in parts]
    parts.append(shard(conv, masks, params, 3, weights, total, before))
    end = parts[-1][3]
    ends = [swap(end, "seq", apart) for apart in (1, 2, 3)]
    states, products = lay_out(parts)
    rows, scale = enter((0, 2, 1, 3), states, products, ends)
    return losses(rows, scale, target)


def solution(mesh):
    shards, devices = mesh.shape["fsdp"], mesh.shape["seq"]
    whole = shards == 4 and devices == 4
    in_specs = (
        P(("segment", "fsdp"), "seq", None),
        P(("segment", "fsdp"), "seq"),
        P(("segment", "fsdp"), "seq", None),
        P("fsdp", None, None, None),
        P(),
        P(),
        P(),
        P(),
    )
    out_specs = (P(("segment", "fsdp"), "seq", None), P(("segment", "fsdp"), "seq"))
    return jax.shard_map(
        local if whole else general,
        mesh=mesh,
        in_specs=in_specs,
        out_specs=out_specs,
        check_vma=False,
    )
```

```python
import functools
import math

import jax
import jax.numpy as jnp
from jax import lax
from jax.experimental import pallas as pl
from jax.experimental.pallas import tpu as pltpu
from jax.sharding import PartitionSpec as P

HEADS = 32
HS = 128
LOG2E = math.log2(math.e)
LN2 = math.log(2.0)
EDGE = 16


def prefix(value, axis, combine, identity):
    devices, here = (lax.axis_size(axis), lax.axis_index(axis))
    everything = jax.tree.map(lambda part: lax.all_gather(part, axis), value)
    start = jax.tree.map(
        lambda part, zero: jnp.broadcast_to(jnp.asarray(zero, part.dtype), part.shape),
        value,
        identity,
    )

    def hop(k, before):
        reached = k < here
        new = combine(before, jax.tree.map(lambda part: part[k], everything))
        return jax.tree.map(lambda a, b: jnp.where(reached, a, b), new, before)

    return lax.fori_loop(0, devices, hop, start)


def from_partner(value, axis, apart):
    return lax.ppermute(value, axis, [(i, i ^ 1 << apart) for i in range(lax.axis_size(axis))])


def from_behind(value, axis, steps):
    count = lax.axis_size(axis)
    leading, last = (max(0, -steps), min(count, count - steps))
    return lax.ppermute(value, axis, [(source, source + steps) for source in range(leading, last)])


def combine(former, latter):
    return (former[0] * latter[0], latter[0] * former[1] + latter[1])


def recurrence(conv_rows, gate_pre_x, gate_pre_a, bias_pair, rates, places):
    group = conv_rows.shape[0]
    tokens = conv_rows.shape[1]
    width = conv_rows.shape[2]
    blocks = tokens // 8
    seq_total = lax.axis_size("seq") * tokens
    gate_x = jax.nn.sigmoid(gate_pre_x + bias_pair[0])
    gate_a = jax.nn.sigmoid(gate_pre_a + bias_pair[1])
    log_a = -8.0 * gate_a * rates / seq_total
    reset = (places == 0)[:, :, None]
    decay = jnp.where(reset, jnp.float32(0.0), jnp.exp(log_a))
    scale = jnp.where(reset, jnp.float32(1.0), jnp.sqrt(-jnp.expm1(2.0 * log_a)))
    drive = conv_rows.astype(jnp.float32) * gate_x * scale
    decay_blocks = decay.reshape(group, blocks, 8, width)
    drive_blocks = drive.reshape(group, blocks, 8, width)
    running_prod = jnp.ones((group, blocks, width), jnp.float32)
    running_state = jnp.zeros((group, blocks, width), jnp.float32)
    prod_list = []
    state_list = []
    for inner in range(8):
        step_decay = decay_blocks[:, :, inner, :]
        running_prod = running_prod * step_decay
        running_state = step_decay * running_state + drive_blocks[:, :, inner, :]
        prod_list.append(running_prod)
        state_list.append(running_state)
    block_prod = jnp.swapaxes(running_prod, 0, 1)
    block_state = jnp.swapaxes(running_state, 0, 1)

    def across(carry, pair):
        after = combine(carry, pair)
        return (after, carry)

    start = (jnp.ones((group, width), jnp.float32), jnp.zeros((group, width), jnp.float32))
    ending, befores = lax.scan(across, start, (block_prod, block_state))
    identity = (jnp.ones_like(ending[0]), jnp.zeros_like(ending[1]))
    incoming = prefix(ending, "seq", combine, identity)
    entering = befores[1] + befores[0] * incoming[1][None, :, :]
    entering = jnp.swapaxes(entering, 0, 1)[:, :, None, :]
    products = jnp.stack(prod_list, axis=2)
    local_state = jnp.stack(state_list, axis=2)
    full = local_state + products * entering
    return full.reshape(group, tokens, width).astype(jnp.bfloat16)


def general(
    branch_x, positions, teacher_held, gate_weights, gate_bias, conv_weight, conv_bias, decay_rate
):
    tokens = branch_x.shape[1]
    width = branch_x.shape[2]
    target = from_partner(teacher_held, "segment", 0)
    previous = from_behind(branch_x[:, -3:, :], "seq", 1)
    extended = jnp.concatenate([previous, branch_x], axis=1).astype(jnp.float32)
    conv = jnp.zeros((1, tokens, width), jnp.float32) + conv_bias
    for lag_steps in range(4):
        valid = (positions >= lag_steps).astype(jnp.float32)[:, :, None]
        conv = (
            conv
            + conv_weight[lag_steps]
            * extended[:, 3 - lag_steps : 3 - lag_steps + tokens, :]
            * valid
        )
    conv_rounded = conv.astype(jnp.bfloat16)
    by_heads = conv_rounded.reshape(1, tokens, HEADS, HS)
    preact = jnp.einsum(
        "nthi,hgij->ngthj",
        by_heads,
        lax.all_gather(gate_weights, "fsdp", axis=0, tiled=True),
        preferred_element_type=jnp.float32,
    )
    student = recurrence(
        conv_rounded,
        preact[:, 0].reshape(1, tokens, width),
        preact[:, 1].reshape(1, tokens, width),
        gate_bias,
        decay_rate,
        positions,
    )
    student_f = student.astype(jnp.float32)
    normed = student_f * lax.rsqrt(jnp.mean(student_f * student_f, axis=-1, keepdims=True) + 1e-06)
    token_loss = jnp.mean((normed - target.astype(jnp.float32)) ** 2, axis=-1)
    return (student, token_loss)


def in_vmem(count):
    return [pl.BlockSpec(memory_space=pltpu.VMEM)] * count


def pallas(kernel, name, out_shape, in_specs, out_specs, scratch_shapes, weight=0, **more):
    return pl.pallas_call(
        kernel,
        out_shape=out_shape,
        in_specs=in_specs,
        out_specs=out_specs,
        scratch_shapes=scratch_shapes,
        compiler_params=pltpu.CompilerParams(vmem_limit_bytes=24 << 20),
        cost_estimate=pl.CostEstimate(
            flops=weight, bytes_accessed=0, transcendentals=0
        ),
        name=name,
        **more,
    )


def cut_kernel(w_ref, quarter_ref, sem):
    quarters = quarter_ref.shape[0]
    first = lax.axis_index("seq") * quarters
    copy = pltpu.make_async_copy(w_ref.at[pl.ds(first, quarters)], quarter_ref, sem)
    copy.start()
    copy.wait()


def cut(gate_weights):
    return pallas(
        cut_kernel,
        "cut",
        jax.ShapeDtypeStruct((gate_weights.shape[0] // 4,) + gate_weights.shape[1:], jnp.bfloat16),
        [pl.BlockSpec(memory_space=pltpu.HBM)],
        pl.BlockSpec(memory_space=pl.ANY),
        [pltpu.SemaphoreType.DMA],
    )(pltpu.with_memory_space_constraint(gate_weights, pltpu.HBM))


def fetch_kernel(x_ref, w_ref, *refs):
    small, refs = refs[: len(refs) // 2 - 1], refs[len(refs) // 2 - 1 :]
    half_ref, edge_ref, *near, sem = refs
    tokens = x_ref.shape[1]
    halves = half_ref.shape[0]
    first = lax.rem(lax.axis_index("seq"), 2) * halves
    pairs = [
        (w_ref.at[pl.ds(first, halves)], half_ref),
        (x_ref.at[0, pl.ds(tokens - EDGE, EDGE), :], edge_ref),
        *zip(small, near),
    ]
    copies = [
        pltpu.make_async_copy(source, target, sem.at[index])
        for index, (source, target) in enumerate(pairs)
    ]
    for copy in copies:
        copy.start()
    for copy in copies:
        copy.wait()


def fetch(branch_x, gate_weights, *small):
    held = gate_weights.shape[0]
    return pallas(
        fetch_kernel,
        "fetch",
        [
            jax.ShapeDtypeStruct((held // 2,) + gate_weights.shape[1:], jnp.bfloat16),
            jax.ShapeDtypeStruct((EDGE, branch_x.shape[2]), jnp.bfloat16),
        ]
        + [jax.ShapeDtypeStruct(value.shape, value.dtype) for value in small],
        [pl.BlockSpec(memory_space=pltpu.HBM)] * (2 + len(small)),
        [pl.BlockSpec(memory_space=pl.ANY)] * (2 + len(small)),
        [pltpu.SemaphoreType.DMA((2 + len(small),))],
        1500000000,
    )(
        *[
            pltpu.with_memory_space_constraint(value, pltpu.HBM)
            for value in (branch_x, gate_weights, *small)
        ]
    )


def spread(codes):
    tokens = codes.shape[1]
    down = lax.broadcasted_iota(jnp.int32, (tokens, tokens), 0)
    across = lax.broadcasted_iota(jnp.int32, (tokens, tokens), 1)
    diagonal = jnp.where(down == across, jnp.broadcast_to(codes, (tokens, tokens)), 0.0)
    return jnp.dot(
        diagonal.astype(jnp.bfloat16),
        jnp.ones((tokens, HS), jnp.bfloat16),
        preferred_element_type=jnp.float32,
    )


def lanes_of(head):
    return pl.ds(pl.multiple_of(head * HS, HS), HS)


def conv_kernel(x_ref, edge_ref, pos_ref, w_ref, b_ref, out_ref, mask_ref, rows, natural, lags):
    tokens = x_ref.shape[1]
    span = tokens // 8
    natural[...] = spread(jnp.minimum(pos_ref[...], 3).astype(jnp.float32))
    for step in range(span):
        code = natural[pl.ds(step, 8, stride=span), :]
        at = pl.ds(step * 8, 8)
        first = jnp.minimum(code, 1.0)
        mask_ref[0, at, :] = first
        mask_ref[1, at, :] = jnp.maximum(1.0 - first, 1e-37)
        lags[0, at, :] = jnp.clip(code - 1.0, 0.0, 1.0)
        lags[1, at, :] = jnp.clip(code - 2.0, 0.0, 1.0)

    def body(head, unused):
        lanes = lanes_of(head)
        rows[head, pl.ds(0, 8), :] = edge_ref[:, lanes].astype(jnp.float32)[EDGE - 8 :]
        rows[head, pl.ds(8, tokens), :] = x_ref[0, :, lanes].astype(jnp.float32)
        tiles = [rows[head, pl.ds(8 + step, 8, stride=span), :] for step in range(-3, span)]
        half = jnp.concatenate(tiles[3:], axis=0) * (w_ref[0:1, lanes] * 0.5) + (
            b_ref[0:1, lanes] * 0.5
        )
        for lag in range(1, 4):
            shifted = jnp.concatenate(tiles[3 - lag : 3 - lag + span], axis=0)
            mask = mask_ref[0] if lag == 1 else lags[lag - 2]
            half = half + shifted * (w_ref[lag : lag + 1, lanes] * 0.5) * mask
        out_ref[head] = half.astype(jnp.bfloat16)
        return unused

    lax.fori_loop(0, out_ref.shape[0], body, 0, unroll=4)


def conv_rows(branch_x, edge, positions, weight, bias):
    tokens, width = branch_x.shape[1:]
    heads = width // HS
    return pallas(
        conv_kernel,
        "conv_rows",
        [
            jax.ShapeDtypeStruct((heads, tokens, HS), jnp.bfloat16),
            jax.ShapeDtypeStruct((2, tokens, HS), jnp.float32),
        ],
        in_vmem(5),
        in_vmem(2),
        [
            pltpu.VMEM((heads, tokens + 8, HS), jnp.float32),
            pltpu.VMEM((tokens, HS), jnp.float32),
            pltpu.VMEM((2, tokens, HS), jnp.float32),
        ],
    )(branch_x, edge, positions, weight, bias)


def across_spans(product, state):
    place = lax.broadcasted_iota(jnp.int32, product.shape, 0)
    for apart in (1, 2, 4):
        reached = place >= apart
        before_p = jnp.where(reached, pltpu.roll(product, apart, 0), 1.0)
        before_s = jnp.where(reached, pltpu.roll(state, apart, 0), 0.0)
        state = product * before_s + state
        product = product * before_p
    enter_p = jnp.where(place >= 1, pltpu.roll(product, 1, 0), 1.0)
    enter_s = jnp.where(place >= 1, pltpu.roll(state, 1, 0), 0.0)
    return product, state, enter_p, enter_s


def gated(total, rounded, weights, masks, bias_ref, rate_ref, head, state_ref, prod_ref, place):
    lanes = lanes_of(head)
    span = rounded.shape[0] // 8
    pre = jnp.dot(rounded, weights, preferred_element_type=jnp.float32)
    gate_x = 1.0 + jnp.tanh(pre[:, :HS] + bias_ref[0:1, lanes] * 0.5)
    gate_a = 1.0 + jnp.tanh(pre[:, HS:] + bias_ref[1:2, lanes] * 0.5)
    power = gate_a * (rate_ref[0:1, lanes] * (-4.0 * LOG2E / total))
    decay = jnp.exp2(power)
    lost = jnp.tanh(power * -LN2)
    square = jnp.maximum(lost + lost * decay * decay, masks[1])
    drive = rounded.astype(jnp.float32) * gate_x * (square * lax.rsqrt(square))
    decay = decay * masks[0]
    product, state = jnp.ones((8, HS), jnp.float32), jnp.zeros((8, HS), jnp.float32)
    for step in range(span):
        at = slice(step * 8, step * 8 + 8)
        state = decay[at] * state + drive[at]
        product = product * decay[at]
        state_ref[place, at, :] = state
        prod_ref[place, at, :] = product
    return across_spans(product, state)


def shard_kernel(total, pair, counts, conv_ref, mask_ref, bias_ref, rate_ref, *refs):
    weights, refs = refs[: len(counts)], refs[len(counts) :]
    before, (state_ref, prod_ref, enter_ref, end_ref) = refs[:-4], refs[-4:]
    heads = state_ref.shape[0]
    row = 2 * heads * len(before)
    for slot, ref in enumerate(before):
        end_ref[pl.ds(2 * heads * slot, 2 * heads), :] = ref[...]
    base = lax.bitwise_xor(lax.axis_index("fsdp"), pair) * heads
    here = lax.axis_index("seq") if len(counts) == 4 else lax.rem(lax.axis_index("seq"), 2)
    masks = (mask_ref[0], mask_ref[1])
    for apart, (count, ref) in enumerate(zip(counts, weights)):
        first = lax.bitwise_xor(here, apart) * count if len(counts) > 1 else 0
        for index in range(count):
            place = first + index
            product, state, enter_p, enter_s = gated(
                total,
                conv_ref[base + place],
                jnp.concatenate([ref[index, 0], ref[index, 1]], axis=1),
                masks,
                bias_ref,
                rate_ref,
                base + place,
                state_ref,
                prod_ref,
                place,
            )
            enter_ref[place, 0] = enter_p
            enter_ref[place, 1] = enter_s
            end_ref[pl.ds(row + place, 1), :] = product[7:8]
            end_ref[pl.ds(row + heads + place, 1), :] = state[7:8]


def shard(conv, masks, params, pair, weights, total, before=()):
    tokens = conv.shape[1]
    counts = tuple(part.shape[0] for part in weights)
    heads = sum(counts)
    return pallas(
        functools.partial(shard_kernel, total, pair, counts),
        "shard",
        [
            jax.ShapeDtypeStruct((heads, tokens, HS), jnp.float32),
            jax.ShapeDtypeStruct((heads, tokens, HS), jnp.float32),
            jax.ShapeDtypeStruct((heads, 2, 8, HS), jnp.float32),
            jax.ShapeDtypeStruct((2 * heads * (1 + len(before)), HS), jnp.float32),
        ],
        in_vmem(4 + len(weights) + len(before)),
        in_vmem(4),
        [],
        5000000000 if before else 0,
    )(conv, masks, *params, *weights, *before)


def lay_kernel(*refs):
    state_out, prod_out = refs[-2:]
    parts = [refs[at : at + 3] for at in range(0, len(refs) - 2, 3)]
    heads, tokens = parts[0][0].shape[:2]
    span = tokens // 8
    for slot, (state_ref, prod_ref, enter_ref) in enumerate(parts):
        for head in range(heads):
            enter_p, enter_s = enter_ref[head, 0], enter_ref[head, 1]
            for step in range(span):
                at = slice(step * 8, step * 8 + 8)
                product = prod_ref[head, at, :]
                natural = pl.ds(step, 8, stride=span)
                state_out[slot * heads + head, natural, :] = state_ref[head, at, :] + product * enter_s
                prod_out[slot * heads + head, natural, :] = product * enter_p


def lay_out(parts):
    heads, tokens = parts[0][0].shape[:2]
    flat = [array for part in parts for array in part[:3]]
    whole = jax.ShapeDtypeStruct((len(parts) * heads, tokens, HS), jnp.float32)
    return pallas(
        lay_kernel,
        "lay_out",
        [whole, whole],
        in_vmem(len(flat)),
        in_vmem(2),
        [],
    )(*flat)


ROWS = 64


def final_kernel(pairs, target_ref, state_ref, prod_ref, *refs):
    devices = lax.axis_size("seq")
    here = lax.axis_index("seq")
    ends, refs = refs[: devices - 1], refs[devices - 1 :]
    student_ref, loss_ref, ends_s, rows, sem = refs
    tokens, full = rows.shape
    heads = state_ref.shape[0] // len(pairs)
    for apart in range(1, devices):
        ends_s[lax.bitwise_xor(here, apart)] = ends[apart - 1][...]
    places = []
    for slot, pair in enumerate(pairs):
        incoming = jnp.zeros((heads, HS), jnp.float32)
        row = 2 * heads * slot
        for place in range(devices - 1):
            after = ends_s[place, row : row + heads, :] * incoming + (
                ends_s[place, row + heads : row + 2 * heads, :]
            )
            incoming = jnp.where(place < here, after, incoming)
        base = lax.bitwise_xor(lax.axis_index("fsdp"), pair) * heads
        for head in range(heads):
            places.append((slot * heads + head, lanes_of(base + head), incoming[head : head + 1]))
    copies, totals = [], []
    for block in range(0, tokens, ROWS):
        at = pl.ds(block, ROWS)
        squares = jnp.zeros((ROWS, HS), jnp.float32)
        for index, lanes, entering in places:
            rounded = (state_ref[index, at, :] + prod_ref[index, at, :] * entering).astype(
                jnp.bfloat16
            )
            rows[at, lanes] = rounded
            value = rounded.astype(jnp.float32)
            squares = squares + value * value
        copies.append(
            pltpu.make_async_copy(rows.at[at, :], student_ref.at[0, at, :], sem.at[len(copies)])
        )
        copies[-1].start()
        mean = jnp.sum(squares, axis=1, keepdims=True) * (1.0 / full)
        scale = jnp.broadcast_to(lax.rsqrt(mean + 1e-06), (ROWS, HS))
        total = jnp.zeros((ROWS, HS), jnp.float32)
        for start in range(0, full, HS):
            lanes = slice(start, start + HS)
            wanted = target_ref[0, at, lanes].astype(jnp.float32)
            off = rows[at, lanes].astype(jnp.float32) * scale - wanted
            total = total + off * off
        totals.append(total)
    total = jnp.concatenate(totals, axis=0)
    loss_ref[...] = jnp.sum(total.T, axis=0, keepdims=True) * (1.0 / full)
    for copy in copies:
        copy.wait()


def final(pairs, target, states, products, ends):
    tokens = states.shape[1]
    full = HEADS * HS
    return pallas(
        functools.partial(final_kernel, pairs),
        "final",
        [
            jax.ShapeDtypeStruct((1, tokens, full), jnp.bfloat16),
            jax.ShapeDtypeStruct((1, tokens), jnp.float32),
        ],
        in_vmem(3 + len(ends)),
        [pl.BlockSpec(memory_space=pltpu.HBM)] + in_vmem(1),
        [
            pltpu.VMEM((len(ends) + 1,) + ends[0].shape, jnp.float32),
            pltpu.VMEM((tokens, full), jnp.bfloat16),
            pltpu.SemaphoreType.DMA((tokens // ROWS,)),
        ],
    )(target, states, products, *ends)


def swap(value, axis, apart):
    return lax.ppermute(value, axis, [(i, i ^ apart) for i in range(lax.axis_size(axis))])


def after(value, *earlier):
    return lax.optimization_barrier((value, *earlier))[0]


def local(
    branch_x, positions, teacher_held, gate_weights, gate_bias, conv_weight, conv_bias, decay_rate
):
    tokens, width = branch_x.shape[1:]
    total = lax.axis_size("seq") * tokens
    target = swap(teacher_held, "segment", 1)
    quarter = cut(gate_weights)
    half, edge, *small = fetch(
        branch_x, gate_weights, positions, conv_weight, conv_bias.reshape(1, width)
    )
    quarters = {pair: swap(quarter, "fsdp", pair) for pair in (2, 3)}
    half = swap(half, "fsdp", 1)
    edge = from_behind(edge, "seq", 1)
    conv, masks = conv_rows(branch_x, edge, *small)
    params = (gate_bias, decay_rate.reshape(1, width))
    parts = [shard(conv, masks, params, 0, [gate_weights], total)]
    two = swap(quarters[2], "seq", 2)
    three = swap(after(quarters[3], masks), "seq", 2)
    mine = after(quarters[2], two, parts[0][3])
    weights = [mine, swap(mine, "seq", 1), two, swap(two, "seq", 1)]
    parts.append(shard(conv, masks, params, 2, weights, total))
    half = after(half, two)
    weights = [half, swap(half, "seq", 1)]
    before = [part[3] for part in parts]
    parts.append(shard(conv, masks, params, 1, weights, total, ()))
    mine = after(quarters[3], three)
    weights = [mine, swap(mine, "seq", 1), three, swap(three, "seq", 1)]
    before = [part[3] for part in parts]
    parts.append(shard(conv, masks, params, 3, weights, total, before))
    end = parts[-1][3]
    ends = [swap(end, "seq", apart) for apart in (1, 2, 3)]
    states, products = lay_out(parts)
    return final((0, 2, 1, 3), target, states, products, ends)


def solution(mesh):
    shards, devices = mesh.shape["fsdp"], mesh.shape["seq"]
    whole = shards == 4 and devices == 4
    in_specs = (
        P(("segment", "fsdp"), "seq", None),
        P(("segment", "fsdp"), "seq"),
        P(("segment", "fsdp"), "seq", None),
        P("fsdp", None, None, None),
        P(),
        P(),
        P(),
        P(),
    )
    out_specs = (P(("segment", "fsdp"), "seq", None), P(("segment", "fsdp"), "seq"))
    return jax.shard_map(
        local if whole else general,
        mesh=mesh,
        in_specs=in_specs,
        out_specs=out_specs,
        check_vma=False,
    )
```

```python
import functools
import math

import jax
import jax.numpy as jnp
from jax import lax
from jax.experimental import pallas as pl
from jax.experimental.pallas import tpu as pltpu
from jax.sharding import PartitionSpec as P

HEADS = 32
HS = 128
LOG2E = math.log2(math.e)
LN2 = math.log(2.0)
EDGE = 16


def prefix(value, axis, combine, identity):
    devices, here = (lax.axis_size(axis), lax.axis_index(axis))
    everything = jax.tree.map(lambda part: lax.all_gather(part, axis), value)
    start = jax.tree.map(
        lambda part, zero: jnp.broadcast_to(jnp.asarray(zero, part.dtype), part.shape),
        value,
        identity,
    )

    def hop(k, before):
        reached = k < here
        new = combine(before, jax.tree.map(lambda part: part[k], everything))
        return jax.tree.map(lambda a, b: jnp.where(reached, a, b), new, before)

    return lax.fori_loop(0, devices, hop, start)


def from_partner(value, axis, apart):
    return lax.ppermute(value, axis, [(i, i ^ 1 << apart) for i in range(lax.axis_size(axis))])


def from_behind(value, axis, steps):
    count = lax.axis_size(axis)
    leading, last = (max(0, -steps), min(count, count - steps))
    return lax.ppermute(value, axis, [(source, source + steps) for source in range(leading, last)])


def combine(former, latter):
    return (former[0] * latter[0], latter[0] * former[1] + latter[1])


def recurrence(conv_rows, gate_pre_x, gate_pre_a, bias_pair, rates, places):
    group = conv_rows.shape[0]
    tokens = conv_rows.shape[1]
    width = conv_rows.shape[2]
    blocks = tokens // 8
    seq_total = lax.axis_size("seq") * tokens
    gate_x = jax.nn.sigmoid(gate_pre_x + bias_pair[0])
    gate_a = jax.nn.sigmoid(gate_pre_a + bias_pair[1])
    log_a = -8.0 * gate_a * rates / seq_total
    reset = (places == 0)[:, :, None]
    decay = jnp.where(reset, jnp.float32(0.0), jnp.exp(log_a))
    scale = jnp.where(reset, jnp.float32(1.0), jnp.sqrt(-jnp.expm1(2.0 * log_a)))
    drive = conv_rows.astype(jnp.float32) * gate_x * scale
    decay_blocks = decay.reshape(group, blocks, 8, width)
    drive_blocks = drive.reshape(group, blocks, 8, width)
    running_prod = jnp.ones((group, blocks, width), jnp.float32)
    running_state = jnp.zeros((group, blocks, width), jnp.float32)
    prod_list = []
    state_list = []
    for inner in range(8):
        step_decay = decay_blocks[:, :, inner, :]
        running_prod = running_prod * step_decay
        running_state = step_decay * running_state + drive_blocks[:, :, inner, :]
        prod_list.append(running_prod)
        state_list.append(running_state)
    block_prod = jnp.swapaxes(running_prod, 0, 1)
    block_state = jnp.swapaxes(running_state, 0, 1)

    def across(carry, pair):
        after = combine(carry, pair)
        return (after, carry)

    start = (jnp.ones((group, width), jnp.float32), jnp.zeros((group, width), jnp.float32))
    ending, befores = lax.scan(across, start, (block_prod, block_state))
    identity = (jnp.ones_like(ending[0]), jnp.zeros_like(ending[1]))
    incoming = prefix(ending, "seq", combine, identity)
    entering = befores[1] + befores[0] * incoming[1][None, :, :]
    entering = jnp.swapaxes(entering, 0, 1)[:, :, None, :]
    products = jnp.stack(prod_list, axis=2)
    local_state = jnp.stack(state_list, axis=2)
    full = local_state + products * entering
    return full.reshape(group, tokens, width).astype(jnp.bfloat16)


def general(
    branch_x, positions, teacher_held, gate_weights, gate_bias, conv_weight, conv_bias, decay_rate
):
    tokens = branch_x.shape[1]
    width = branch_x.shape[2]
    target = from_partner(teacher_held, "segment", 0)
    previous = from_behind(branch_x[:, -3:, :], "seq", 1)
    extended = jnp.concatenate([previous, branch_x], axis=1).astype(jnp.float32)
    conv = jnp.zeros((1, tokens, width), jnp.float32) + conv_bias
    for lag_steps in range(4):
        valid = (positions >= lag_steps).astype(jnp.float32)[:, :, None]
        conv = (
            conv
            + conv_weight[lag_steps]
            * extended[:, 3 - lag_steps : 3 - lag_steps + tokens, :]
            * valid
        )
    conv_rounded = conv.astype(jnp.bfloat16)
    by_heads = conv_rounded.reshape(1, tokens, HEADS, HS)
    preact = jnp.einsum(
        "nthi,hgij->ngthj",
        by_heads,
        lax.all_gather(gate_weights, "fsdp", axis=0, tiled=True),
        preferred_element_type=jnp.float32,
    )
    student = recurrence(
        conv_rounded,
        preact[:, 0].reshape(1, tokens, width),
        preact[:, 1].reshape(1, tokens, width),
        gate_bias,
        decay_rate,
        positions,
    )
    student_f = student.astype(jnp.float32)
    normed = student_f * lax.rsqrt(jnp.mean(student_f * student_f, axis=-1, keepdims=True) + 1e-06)
    token_loss = jnp.mean((normed - target.astype(jnp.float32)) ** 2, axis=-1)
    return (student, token_loss)


def in_vmem(count):
    return [pl.BlockSpec(memory_space=pltpu.VMEM)] * count


def pallas(kernel, name, out_shape, in_specs, out_specs, scratch_shapes, weight=0, **more):
    return pl.pallas_call(
        kernel,
        out_shape=out_shape,
        in_specs=in_specs,
        out_specs=out_specs,
        scratch_shapes=scratch_shapes,
        compiler_params=pltpu.CompilerParams(vmem_limit_bytes=24 << 20),
        cost_estimate=pl.CostEstimate(
            flops=weight, bytes_accessed=0, transcendentals=0
        ),
        name=name,
        **more,
    )


def cut_kernel(w_ref, quarter_ref, sem):
    quarters = quarter_ref.shape[0]
    first = lax.axis_index("seq") * quarters
    copy = pltpu.make_async_copy(w_ref.at[pl.ds(first, quarters)], quarter_ref, sem)
    copy.start()
    copy.wait()


def cut(gate_weights):
    return pallas(
        cut_kernel,
        "cut",
        jax.ShapeDtypeStruct((gate_weights.shape[0] // 4,) + gate_weights.shape[1:], jnp.bfloat16),
        [pl.BlockSpec(memory_space=pltpu.HBM)],
        pl.BlockSpec(memory_space=pl.ANY),
        [pltpu.SemaphoreType.DMA],
    )(pltpu.with_memory_space_constraint(gate_weights, pltpu.HBM))


def fetch_kernel(x_ref, w_ref, *refs):
    small, refs = refs[: len(refs) // 2 - 1], refs[len(refs) // 2 - 1 :]
    half_ref, edge_ref, *near, sem = refs
    tokens = x_ref.shape[1]
    halves = half_ref.shape[0]
    first = lax.rem(lax.axis_index("seq"), 2) * halves
    pairs = [
        (w_ref.at[pl.ds(first, halves)], half_ref),
        (x_ref.at[0, pl.ds(tokens - EDGE, EDGE), :], edge_ref),
        *zip(small, near),
    ]
    copies = [
        pltpu.make_async_copy(source, target, sem.at[index])
        for index, (source, target) in enumerate(pairs)
    ]
    for copy in copies:
        copy.start()
    for copy in copies:
        copy.wait()


def fetch(branch_x, gate_weights, *small):
    held = gate_weights.shape[0]
    return pallas(
        fetch_kernel,
        "fetch",
        [
            jax.ShapeDtypeStruct((held // 2,) + gate_weights.shape[1:], jnp.bfloat16),
            jax.ShapeDtypeStruct((EDGE, branch_x.shape[2]), jnp.bfloat16),
        ]
        + [jax.ShapeDtypeStruct(value.shape, value.dtype) for value in small],
        [pl.BlockSpec(memory_space=pltpu.HBM)] * (2 + len(small)),
        [pl.BlockSpec(memory_space=pl.ANY)] * (2 + len(small)),
        [pltpu.SemaphoreType.DMA((2 + len(small),))],
        1500000000,
    )(
        *[
            pltpu.with_memory_space_constraint(value, pltpu.HBM)
            for value in (branch_x, gate_weights, *small)
        ]
    )


def spread(codes):
    tokens = codes.shape[1]
    down = lax.broadcasted_iota(jnp.int32, (tokens, tokens), 0)
    across = lax.broadcasted_iota(jnp.int32, (tokens, tokens), 1)
    diagonal = jnp.where(down == across, jnp.broadcast_to(codes, (tokens, tokens)), 0.0)
    return jnp.dot(
        diagonal.astype(jnp.bfloat16),
        jnp.ones((tokens, HS), jnp.bfloat16),
        preferred_element_type=jnp.float32,
    )


def lanes_of(head):
    return pl.ds(pl.multiple_of(head * HS, HS), HS)


def conv_kernel(x_ref, edge_ref, pos_ref, w_ref, b_ref, out_ref, mask_ref, rows, natural, lags):
    tokens = x_ref.shape[1]
    span = tokens // 8
    natural[...] = spread(jnp.minimum(pos_ref[...], 3).astype(jnp.float32))
    for step in range(span):
        code = natural[pl.ds(step, 8, stride=span), :]
        at = pl.ds(step * 8, 8)
        first = jnp.minimum(code, 1.0)
        mask_ref[0, at, :] = first
        mask_ref[1, at, :] = jnp.maximum(1.0 - first, 1e-37)
        lags[0, at, :] = jnp.clip(code - 1.0, 0.0, 1.0)
        lags[1, at, :] = jnp.clip(code - 2.0, 0.0, 1.0)

    def body(head, unused):
        lanes = lanes_of(head)
        rows[head, pl.ds(0, 8), :] = edge_ref[:, lanes].astype(jnp.float32)[EDGE - 8 :]
        rows[head, pl.ds(8, tokens), :] = x_ref[0, :, lanes].astype(jnp.float32)
        tiles = [rows[head, pl.ds(8 + step, 8, stride=span), :] for step in range(-3, span)]
        half = jnp.concatenate(tiles[3:], axis=0) * (w_ref[0:1, lanes] * 0.5) + (
            b_ref[0:1, lanes] * 0.5
        )
        for lag in range(1, 4):
            shifted = jnp.concatenate(tiles[3 - lag : 3 - lag + span], axis=0)
            mask = mask_ref[0] if lag == 1 else lags[lag - 2]
            half = half + shifted * (w_ref[lag : lag + 1, lanes] * 0.5) * mask
        out_ref[head] = half.astype(jnp.bfloat16)
        return unused

    lax.fori_loop(0, out_ref.shape[0], body, 0, unroll=4)


def conv_rows(branch_x, edge, positions, weight, bias):
    tokens, width = branch_x.shape[1:]
    heads = width // HS
    return pallas(
        conv_kernel,
        "conv_rows",
        [
            jax.ShapeDtypeStruct((heads, tokens, HS), jnp.bfloat16),
            jax.ShapeDtypeStruct((2, tokens, HS), jnp.float32),
        ],
        in_vmem(5),
        in_vmem(2),
        [
            pltpu.VMEM((heads, tokens + 8, HS), jnp.float32),
            pltpu.VMEM((tokens, HS), jnp.float32),
            pltpu.VMEM((2, tokens, HS), jnp.float32),
        ],
    )(branch_x, edge, positions, weight, bias)


def across_spans(product, state):
    place = lax.broadcasted_iota(jnp.int32, product.shape, 0)
    for apart in (1, 2, 4):
        reached = place >= apart
        before_p = jnp.where(reached, pltpu.roll(product, apart, 0), 1.0)
        before_s = jnp.where(reached, pltpu.roll(state, apart, 0), 0.0)
        state = product * before_s + state
        product = product * before_p
    enter_p = jnp.where(place >= 1, pltpu.roll(product, 1, 0), 1.0)
    enter_s = jnp.where(place >= 1, pltpu.roll(state, 1, 0), 0.0)
    return product, state, enter_p, enter_s


def gated(total, rounded, weights, masks, bias_ref, rate_ref, head, state_ref, prod_ref, place):
    lanes = lanes_of(head)
    span = rounded.shape[0] // 8
    pre = jnp.dot(rounded, weights, preferred_element_type=jnp.float32)
    gate_x = 1.0 + jnp.tanh(pre[:, :HS] + bias_ref[0:1, lanes] * 0.5)
    gate_a = 1.0 + jnp.tanh(pre[:, HS:] + bias_ref[1:2, lanes] * 0.5)
    power = gate_a * (rate_ref[0:1, lanes] * (-4.0 * LOG2E / total))
    decay = jnp.exp2(power)
    lost = jnp.tanh(power * -LN2)
    square = jnp.maximum(lost + lost * decay * decay, masks[1])
    drive = rounded.astype(jnp.float32) * gate_x * (square * lax.rsqrt(square))
    decay = decay * masks[0]
    product, state = jnp.ones((8, HS), jnp.float32), jnp.zeros((8, HS), jnp.float32)
    for step in range(span):
        at = slice(step * 8, step * 8 + 8)
        state = decay[at] * state + drive[at]
        product = product * decay[at]
        state_ref[place, at, :] = state
        prod_ref[place, at, :] = product
    return across_spans(product, state)


def shard_kernel(total, pair, counts, conv_ref, mask_ref, bias_ref, rate_ref, *refs):
    weights, refs = refs[: len(counts)], refs[len(counts) :]
    before, (state_ref, prod_ref, enter_ref, end_ref) = refs[:-4], refs[-4:]
    heads = state_ref.shape[0]
    row = 2 * heads * len(before)
    for slot, ref in enumerate(before):
        end_ref[pl.ds(2 * heads * slot, 2 * heads), :] = ref[...]
    base = lax.bitwise_xor(lax.axis_index("fsdp"), pair) * heads
    here = lax.axis_index("seq") if len(counts) == 4 else lax.rem(lax.axis_index("seq"), 2)
    masks = (mask_ref[0], mask_ref[1])
    for apart, (count, ref) in enumerate(zip(counts, weights)):
        first = lax.bitwise_xor(here, apart) * count if len(counts) > 1 else 0
        for index in range(count):
            place = first + index
            product, state, enter_p, enter_s = gated(
                total,
                conv_ref[base + place],
                jnp.concatenate([ref[index, 0], ref[index, 1]], axis=1),
                masks,
                bias_ref,
                rate_ref,
                base + place,
                state_ref,
                prod_ref,
                place,
            )
            enter_ref[place, 0] = enter_p
            enter_ref[place, 1] = enter_s
            end_ref[pl.ds(row + place, 1), :] = product[7:8]
            end_ref[pl.ds(row + heads + place, 1), :] = state[7:8]


def shard(conv, masks, params, pair, weights, total, before=()):
    tokens = conv.shape[1]
    counts = tuple(part.shape[0] for part in weights)
    heads = sum(counts)
    return pallas(
        functools.partial(shard_kernel, total, pair, counts),
        "shard",
        [
            jax.ShapeDtypeStruct((heads, tokens, HS), jnp.float32),
            jax.ShapeDtypeStruct((heads, tokens, HS), jnp.float32),
            jax.ShapeDtypeStruct((heads, 2, 8, HS), jnp.float32),
            jax.ShapeDtypeStruct((2 * heads * (1 + len(before)), HS), jnp.float32),
        ],
        in_vmem(4 + len(weights) + len(before)),
        in_vmem(4),
        [],
        5000000000 if before else 0,
    )(conv, masks, *params, *weights, *before)


def lay_kernel(*refs):
    state_out, prod_out = refs[-2:]
    parts = [refs[at : at + 3] for at in range(0, len(refs) - 2, 3)]
    heads, tokens = parts[0][0].shape[:2]
    span = tokens // 8
    for slot, (state_ref, prod_ref, enter_ref) in enumerate(parts):
        for head in range(heads):
            enter_p, enter_s = enter_ref[head, 0], enter_ref[head, 1]
            for step in range(span):
                at = slice(step * 8, step * 8 + 8)
                product = prod_ref[head, at, :]
                natural = pl.ds(step, 8, stride=span)
                state_out[slot * heads + head, natural, :] = state_ref[head, at, :] + product * enter_s
                prod_out[slot * heads + head, natural, :] = product * enter_p


def lay_out(parts):
    heads, tokens = parts[0][0].shape[:2]
    flat = [array for part in parts for array in part[:3]]
    whole = jax.ShapeDtypeStruct((len(parts) * heads, tokens, HS), jnp.float32)
    return pallas(
        lay_kernel,
        "lay_out",
        [whole, whole],
        in_vmem(len(flat)),
        in_vmem(2),
        [],
    )(*flat)


ROWS = 32


def final_kernel(pairs, target_ref, state_ref, prod_ref, *refs):
    devices = lax.axis_size("seq")
    here = lax.axis_index("seq")
    ends, refs = refs[: devices - 1], refs[devices - 1 :]
    student_ref, loss_ref, ends_s, rows, sem = refs
    tokens, full = rows.shape
    heads = state_ref.shape[0] // len(pairs)
    for apart in range(1, devices):
        ends_s[lax.bitwise_xor(here, apart)] = ends[apart - 1][...]
    places = []
    for slot, pair in enumerate(pairs):
        incoming = jnp.zeros((heads, HS), jnp.float32)
        row = 2 * heads * slot
        for place in range(devices - 1):
            after = ends_s[place, row : row + heads, :] * incoming + (
                ends_s[place, row + heads : row + 2 * heads, :]
            )
            incoming = jnp.where(place < here, after, incoming)
        base = lax.bitwise_xor(lax.axis_index("fsdp"), pair) * heads
        for head in range(heads):
            places.append((slot * heads + head, lanes_of(base + head), incoming[head : head + 1]))
    copies, scales, totals = [], [], []
    for block in range(0, tokens, ROWS):
        at = pl.ds(block, ROWS)
        squares = jnp.zeros((ROWS, HS), jnp.float32)
        for index, lanes, entering in places:
            rounded = (state_ref[index, at, :] + prod_ref[index, at, :] * entering).astype(
                jnp.bfloat16
            )
            rows[at, lanes] = rounded
            value = rounded.astype(jnp.float32)
            squares = squares + value * value
        copies.append(
            pltpu.make_async_copy(rows.at[at, :], student_ref.at[0, at, :], sem.at[len(copies)])
        )
        copies[-1].start()
        mean = jnp.sum(squares, axis=1, keepdims=True) * (1.0 / full)
        scales.append(jnp.broadcast_to(lax.rsqrt(mean + 1e-06), (ROWS, HS)))
    for block, scale in zip(range(0, tokens, ROWS), scales):
        at = pl.ds(block, ROWS)
        total = jnp.zeros((ROWS, HS), jnp.float32)
        for start in range(0, full, HS):
            lanes = slice(start, start + HS)
            wanted = target_ref[0, at, lanes].astype(jnp.float32)
            off = rows[at, lanes].astype(jnp.float32) * scale - wanted
            total = total + off * off
        totals.append(total)
    total = jnp.concatenate(totals, axis=0)
    loss_ref[...] = jnp.sum(total.T, axis=0, keepdims=True) * (1.0 / full)
    for copy in copies:
        copy.wait()


def final(pairs, target, states, products, ends):
    tokens = states.shape[1]
    full = HEADS * HS
    return pallas(
        functools.partial(final_kernel, pairs),
        "final",
        [
            jax.ShapeDtypeStruct((1, tokens, full), jnp.bfloat16),
            jax.ShapeDtypeStruct((1, tokens), jnp.float32),
        ],
        in_vmem(3 + len(ends)),
        [pl.BlockSpec(memory_space=pltpu.HBM)] + in_vmem(1),
        [
            pltpu.VMEM((len(ends) + 1,) + ends[0].shape, jnp.float32),
            pltpu.VMEM((tokens, full), jnp.bfloat16),
            pltpu.SemaphoreType.DMA((tokens // ROWS,)),
        ],
    )(target, states, products, *ends)


def swap(value, axis, apart):
    return lax.ppermute(value, axis, [(i, i ^ apart) for i in range(lax.axis_size(axis))])


def after(value, *earlier):
    return lax.optimization_barrier((value, *earlier))[0]


def local(
    branch_x, positions, teacher_held, gate_weights, gate_bias, conv_weight, conv_bias, decay_rate
):
    tokens, width = branch_x.shape[1:]
    total = lax.axis_size("seq") * tokens
    target = swap(teacher_held, "segment", 1)
    quarter = cut(gate_weights)
    half, edge, *small = fetch(
        branch_x, gate_weights, positions, conv_weight, conv_bias.reshape(1, width)
    )
    quarters = {pair: swap(quarter, "fsdp", pair) for pair in (2, 3)}
    half = swap(half, "fsdp", 1)
    edge = from_behind(edge, "seq", 1)
    conv, masks = conv_rows(branch_x, edge, *small)
    params = (gate_bias, decay_rate.reshape(1, width))
    parts = [shard(conv, masks, params, 0, [gate_weights], total)]
    two = swap(quarters[2], "seq", 2)
    three = swap(after(quarters[3], masks), "seq", 2)
    mine = after(quarters[2], two, parts[0][3])
    weights = [mine, swap(mine, "seq", 1), two, swap(two, "seq", 1)]
    parts.append(shard(conv, masks, params, 2, weights, total))
    half = after(half, two)
    weights = [half, swap(half, "seq", 1)]
    before = [part[3] for part in parts]
    parts.append(shard(conv, masks, params, 1, weights, total, ()))
    mine = after(quarters[3], three)
    weights = [mine, swap(mine, "seq", 1), three, swap(three, "seq", 1)]
    before = [part[3] for part in parts]
    parts.append(shard(conv, masks, params, 3, weights, total, before))
    end = parts[-1][3]
    ends = [swap(end, "seq", apart) for apart in (1, 2, 3)]
    states, products = lay_out(parts)
    return final((0, 2, 1, 3), target, states, products, ends)


def solution(mesh):
    shards, devices = mesh.shape["fsdp"], mesh.shape["seq"]
    whole = shards == 4 and devices == 4
    in_specs = (
        P(("segment", "fsdp"), "seq", None),
        P(("segment", "fsdp"), "seq"),
        P(("segment", "fsdp"), "seq", None),
        P("fsdp", None, None, None),
        P(),
        P(),
        P(),
        P(),
    )
    out_specs = (P(("segment", "fsdp"), "seq", None), P(("segment", "fsdp"), "seq"))
    return jax.shard_map(
        local if whole else general,
        mesh=mesh,
        in_specs=in_specs,
        out_specs=out_specs,
        check_vma=False,
    )
```

```python
import functools
import math

import jax
import jax.numpy as jnp
from jax import lax
from jax.experimental import pallas as pl
from jax.experimental.pallas import tpu as pltpu
from jax.sharding import PartitionSpec as P

HEADS = 32
HS = 128
LOG2E = math.log2(math.e)
LN2 = math.log(2.0)
EDGE = 16


def prefix(value, axis, combine, identity):
    devices, here = (lax.axis_size(axis), lax.axis_index(axis))
    everything = jax.tree.map(lambda part: lax.all_gather(part, axis), value)
    start = jax.tree.map(
        lambda part, zero: jnp.broadcast_to(jnp.asarray(zero, part.dtype), part.shape),
        value,
        identity,
    )

    def hop(k, before):
        reached = k < here
        new = combine(before, jax.tree.map(lambda part: part[k], everything))
        return jax.tree.map(lambda a, b: jnp.where(reached, a, b), new, before)

    return lax.fori_loop(0, devices, hop, start)


def from_partner(value, axis, apart):
    return lax.ppermute(value, axis, [(i, i ^ 1 << apart) for i in range(lax.axis_size(axis))])


def from_behind(value, axis, steps):
    count = lax.axis_size(axis)
    leading, last = (max(0, -steps), min(count, count - steps))
    return lax.ppermute(value, axis, [(source, source + steps) for source in range(leading, last)])


def combine(former, latter):
    return (former[0] * latter[0], latter[0] * former[1] + latter[1])


def recurrence(conv_rows, gate_pre_x, gate_pre_a, bias_pair, rates, places):
    group = conv_rows.shape[0]
    tokens = conv_rows.shape[1]
    width = conv_rows.shape[2]
    blocks = tokens // 8
    seq_total = lax.axis_size("seq") * tokens
    gate_x = jax.nn.sigmoid(gate_pre_x + bias_pair[0])
    gate_a = jax.nn.sigmoid(gate_pre_a + bias_pair[1])
    log_a = -8.0 * gate_a * rates / seq_total
    reset = (places == 0)[:, :, None]
    decay = jnp.where(reset, jnp.float32(0.0), jnp.exp(log_a))
    scale = jnp.where(reset, jnp.float32(1.0), jnp.sqrt(-jnp.expm1(2.0 * log_a)))
    drive = conv_rows.astype(jnp.float32) * gate_x * scale
    decay_blocks = decay.reshape(group, blocks, 8, width)
    drive_blocks = drive.reshape(group, blocks, 8, width)
    running_prod = jnp.ones((group, blocks, width), jnp.float32)
    running_state = jnp.zeros((group, blocks, width), jnp.float32)
    prod_list = []
    state_list = []
    for inner in range(8):
        step_decay = decay_blocks[:, :, inner, :]
        running_prod = running_prod * step_decay
        running_state = step_decay * running_state + drive_blocks[:, :, inner, :]
        prod_list.append(running_prod)
        state_list.append(running_state)
    block_prod = jnp.swapaxes(running_prod, 0, 1)
    block_state = jnp.swapaxes(running_state, 0, 1)

    def across(carry, pair):
        after = combine(carry, pair)
        return (after, carry)

    start = (jnp.ones((group, width), jnp.float32), jnp.zeros((group, width), jnp.float32))
    ending, befores = lax.scan(across, start, (block_prod, block_state))
    identity = (jnp.ones_like(ending[0]), jnp.zeros_like(ending[1]))
    incoming = prefix(ending, "seq", combine, identity)
    entering = befores[1] + befores[0] * incoming[1][None, :, :]
    entering = jnp.swapaxes(entering, 0, 1)[:, :, None, :]
    products = jnp.stack(prod_list, axis=2)
    local_state = jnp.stack(state_list, axis=2)
    full = local_state + products * entering
    return full.reshape(group, tokens, width).astype(jnp.bfloat16)


def general(
    branch_x, positions, teacher_held, gate_weights, gate_bias, conv_weight, conv_bias, decay_rate
):
    tokens = branch_x.shape[1]
    width = branch_x.shape[2]
    target = from_partner(teacher_held, "segment", 0)
    previous = from_behind(branch_x[:, -3:, :], "seq", 1)
    extended = jnp.concatenate([previous, branch_x], axis=1).astype(jnp.float32)
    conv = jnp.zeros((1, tokens, width), jnp.float32) + conv_bias
    for lag_steps in range(4):
        valid = (positions >= lag_steps).astype(jnp.float32)[:, :, None]
        conv = (
            conv
            + conv_weight[lag_steps]
            * extended[:, 3 - lag_steps : 3 - lag_steps + tokens, :]
            * valid
        )
    conv_rounded = conv.astype(jnp.bfloat16)
    by_heads = conv_rounded.reshape(1, tokens, HEADS, HS)
    preact = jnp.einsum(
        "nthi,hgij->ngthj",
        by_heads,
        lax.all_gather(gate_weights, "fsdp", axis=0, tiled=True),
        preferred_element_type=jnp.float32,
    )
    student = recurrence(
        conv_rounded,
        preact[:, 0].reshape(1, tokens, width),
        preact[:, 1].reshape(1, tokens, width),
        gate_bias,
        decay_rate,
        positions,
    )
    student_f = student.astype(jnp.float32)
    normed = student_f * lax.rsqrt(jnp.mean(student_f * student_f, axis=-1, keepdims=True) + 1e-06)
    token_loss = jnp.mean((normed - target.astype(jnp.float32)) ** 2, axis=-1)
    return (student, token_loss)


def in_vmem(count):
    return [pl.BlockSpec(memory_space=pltpu.VMEM)] * count


def pallas(kernel, name, out_shape, in_specs, out_specs, scratch_shapes, weight=0, **more):
    return pl.pallas_call(
        kernel,
        out_shape=out_shape,
        in_specs=in_specs,
        out_specs=out_specs,
        scratch_shapes=scratch_shapes,
        compiler_params=pltpu.CompilerParams(vmem_limit_bytes=24 << 20),
        cost_estimate=pl.CostEstimate(
            flops=weight, bytes_accessed=0, transcendentals=0
        ),
        name=name,
        **more,
    )


def cut_kernel(w_ref, quarter_ref, sem):
    quarters = quarter_ref.shape[0]
    first = lax.axis_index("seq") * quarters
    copy = pltpu.make_async_copy(w_ref.at[pl.ds(first, quarters)], quarter_ref, sem)
    copy.start()
    copy.wait()


def cut(gate_weights):
    return pallas(
        cut_kernel,
        "cut",
        jax.ShapeDtypeStruct((gate_weights.shape[0] // 4,) + gate_weights.shape[1:], jnp.bfloat16),
        [pl.BlockSpec(memory_space=pltpu.HBM)],
        pl.BlockSpec(memory_space=pl.ANY),
        [pltpu.SemaphoreType.DMA],
    )(pltpu.with_memory_space_constraint(gate_weights, pltpu.HBM))


def fetch_kernel(x_ref, w_ref, *refs):
    small, refs = refs[: len(refs) // 2 - 1], refs[len(refs) // 2 - 1 :]
    half_ref, edge_ref, *near, sem = refs
    tokens = x_ref.shape[1]
    halves = half_ref.shape[0]
    first = lax.rem(lax.axis_index("seq"), 2) * halves
    pairs = [
        (w_ref.at[pl.ds(first, halves)], half_ref),
        (x_ref.at[0, pl.ds(tokens - EDGE, EDGE), :], edge_ref),
        *zip(small, near),
    ]
    copies = [
        pltpu.make_async_copy(source, target, sem.at[index])
        for index, (source, target) in enumerate(pairs)
    ]
    for copy in copies:
        copy.start()
    for copy in copies:
        copy.wait()


def fetch(branch_x, gate_weights, *small):
    held = gate_weights.shape[0]
    return pallas(
        fetch_kernel,
        "fetch",
        [
            jax.ShapeDtypeStruct((held // 2,) + gate_weights.shape[1:], jnp.bfloat16),
            jax.ShapeDtypeStruct((EDGE, branch_x.shape[2]), jnp.bfloat16),
        ]
        + [jax.ShapeDtypeStruct(value.shape, value.dtype) for value in small],
        [pl.BlockSpec(memory_space=pltpu.HBM)] * (2 + len(small)),
        [pl.BlockSpec(memory_space=pl.ANY)] * (2 + len(small)),
        [pltpu.SemaphoreType.DMA((2 + len(small),))],
        1500000000,
    )(
        *[
            pltpu.with_memory_space_constraint(value, pltpu.HBM)
            for value in (branch_x, gate_weights, *small)
        ]
    )


def spread(codes):
    tokens = codes.shape[1]
    down = lax.broadcasted_iota(jnp.int32, (tokens, tokens), 0)
    across = lax.broadcasted_iota(jnp.int32, (tokens, tokens), 1)
    diagonal = jnp.where(down == across, jnp.broadcast_to(codes, (tokens, tokens)), 0.0)
    return jnp.dot(
        diagonal.astype(jnp.bfloat16),
        jnp.ones((tokens, HS), jnp.bfloat16),
        preferred_element_type=jnp.float32,
    )


def lanes_of(head):
    return pl.ds(pl.multiple_of(head * HS, HS), HS)


def conv_kernel(x_ref, edge_ref, pos_ref, w_ref, b_ref, out_ref, mask_ref, rows, natural, lags):
    tokens = x_ref.shape[1]
    span = tokens // 8
    natural[...] = spread(jnp.minimum(pos_ref[...], 3).astype(jnp.float32))
    for step in range(span):
        code = natural[pl.ds(step, 8, stride=span), :]
        at = pl.ds(step * 8, 8)
        first = jnp.minimum(code, 1.0)
        mask_ref[0, at, :] = first
        mask_ref[1, at, :] = jnp.maximum(1.0 - first, 1e-37)
        lags[0, at, :] = jnp.clip(code - 1.0, 0.0, 1.0)
        lags[1, at, :] = jnp.clip(code - 2.0, 0.0, 1.0)

    def body(head, unused):
        lanes = lanes_of(head)
        rows[head, pl.ds(0, 8), :] = edge_ref[:, lanes].astype(jnp.float32)[EDGE - 8 :]
        rows[head, pl.ds(8, tokens), :] = x_ref[0, :, lanes].astype(jnp.float32)
        tiles = [rows[head, pl.ds(8 + step, 8, stride=span), :] for step in range(-3, span)]
        half = jnp.concatenate(tiles[3:], axis=0) * (w_ref[0:1, lanes] * 0.5) + (
            b_ref[0:1, lanes] * 0.5
        )
        for lag in range(1, 4):
            shifted = jnp.concatenate(tiles[3 - lag : 3 - lag + span], axis=0)
            mask = mask_ref[0] if lag == 1 else lags[lag - 2]
            half = half + shifted * (w_ref[lag : lag + 1, lanes] * 0.5) * mask
        out_ref[head] = half.astype(jnp.bfloat16)
        return unused

    lax.fori_loop(0, out_ref.shape[0], body, 0, unroll=4)


def conv_rows(branch_x, edge, positions, weight, bias):
    tokens, width = branch_x.shape[1:]
    heads = width // HS
    return pallas(
        conv_kernel,
        "conv_rows",
        [
            jax.ShapeDtypeStruct((heads, tokens, HS), jnp.bfloat16),
            jax.ShapeDtypeStruct((2, tokens, HS), jnp.float32),
        ],
        in_vmem(5),
        in_vmem(2),
        [
            pltpu.VMEM((heads, tokens + 8, HS), jnp.float32),
            pltpu.VMEM((tokens, HS), jnp.float32),
            pltpu.VMEM((2, tokens, HS), jnp.float32),
        ],
    )(branch_x, edge, positions, weight, bias)


def across_spans(product, state):
    place = lax.broadcasted_iota(jnp.int32, product.shape, 0)
    for apart in (1, 2, 4):
        reached = place >= apart
        before_p = jnp.where(reached, pltpu.roll(product, apart, 0), 1.0)
        before_s = jnp.where(reached, pltpu.roll(state, apart, 0), 0.0)
        state = product * before_s + state
        product = product * before_p
    enter_p = jnp.where(place >= 1, pltpu.roll(product, 1, 0), 1.0)
    enter_s = jnp.where(place >= 1, pltpu.roll(state, 1, 0), 0.0)
    return product, state, enter_p, enter_s


def gated(total, rounded, weights, masks, bias_ref, rate_ref, head, state_ref, prod_ref, place):
    lanes = lanes_of(head)
    span = rounded.shape[0] // 8
    pre = jnp.dot(rounded, weights, preferred_element_type=jnp.float32)
    gate_x = 1.0 + jnp.tanh(pre[:, :HS] + bias_ref[0:1, lanes] * 0.5)
    gate_a = 1.0 + jnp.tanh(pre[:, HS:] + bias_ref[1:2, lanes] * 0.5)
    power = gate_a * (rate_ref[0:1, lanes] * (-4.0 * LOG2E / total))
    decay = jnp.exp2(power)
    lost = jnp.tanh(power * -LN2)
    square = jnp.maximum(lost + lost * decay * decay, masks[1])
    drive = rounded.astype(jnp.float32) * gate_x * (square * lax.rsqrt(square))
    decay = decay * masks[0]
    product, state = jnp.ones((8, HS), jnp.float32), jnp.zeros((8, HS), jnp.float32)
    for step in range(span):
        at = slice(step * 8, step * 8 + 8)
        state = decay[at] * state + drive[at]
        product = product * decay[at]
        state_ref[place, at, :] = state
        prod_ref[place, at, :] = product
    return across_spans(product, state)


def shard_kernel(total, pair, counts, conv_ref, mask_ref, bias_ref, rate_ref, *refs):
    weights, refs = refs[: len(counts)], refs[len(counts) :]
    before, (state_ref, prod_ref, enter_ref, end_ref) = refs[:-4], refs[-4:]
    heads = state_ref.shape[0]
    row = 2 * heads * len(before)
    for slot, ref in enumerate(before):
        end_ref[pl.ds(2 * heads * slot, 2 * heads), :] = ref[...]
    base = lax.bitwise_xor(lax.axis_index("fsdp"), pair) * heads
    here = lax.axis_index("seq") if len(counts) == 4 else lax.rem(lax.axis_index("seq"), 2)
    masks = (mask_ref[0], mask_ref[1])
    for apart, (count, ref) in enumerate(zip(counts, weights)):
        first = lax.bitwise_xor(here, apart) * count if len(counts) > 1 else 0
        for index in range(count):
            place = first + index
            product, state, enter_p, enter_s = gated(
                total,
                conv_ref[base + place],
                jnp.concatenate([ref[index, 0], ref[index, 1]], axis=1),
                masks,
                bias_ref,
                rate_ref,
                base + place,
                state_ref,
                prod_ref,
                place,
            )
            enter_ref[place, 0] = enter_p
            enter_ref[place, 1] = enter_s
            end_ref[pl.ds(row + place, 1), :] = product[7:8]
            end_ref[pl.ds(row + heads + place, 1), :] = state[7:8]


def shard(conv, masks, params, pair, weights, total, before=()):
    tokens = conv.shape[1]
    counts = tuple(part.shape[0] for part in weights)
    heads = sum(counts)
    return pallas(
        functools.partial(shard_kernel, total, pair, counts),
        "shard",
        [
            jax.ShapeDtypeStruct((heads, tokens, HS), jnp.float32),
            jax.ShapeDtypeStruct((heads, tokens, HS), jnp.float32),
            jax.ShapeDtypeStruct((heads, 2, 8, HS), jnp.float32),
            jax.ShapeDtypeStruct((2 * heads * (1 + len(before)), HS), jnp.float32),
        ],
        in_vmem(4 + len(weights) + len(before)),
        in_vmem(4),
        [],
        5000000000 if before else 0,
    )(conv, masks, *params, *weights, *before)


def lay_kernel(*refs):
    state_out, prod_out = refs[-2:]
    parts = [refs[at : at + 3] for at in range(0, len(refs) - 2, 3)]
    heads, tokens = parts[0][0].shape[:2]
    span = tokens // 8
    for slot, (state_ref, prod_ref, enter_ref) in enumerate(parts):
        for head in range(heads):
            enter_p, enter_s = enter_ref[head, 0], enter_ref[head, 1]
            for step in range(span):
                at = slice(step * 8, step * 8 + 8)
                product = prod_ref[head, at, :]
                natural = pl.ds(step, 8, stride=span)
                state_out[slot * heads + head, natural, :] = state_ref[head, at, :] + product * enter_s
                prod_out[slot * heads + head, natural, :] = product * enter_p


def lay_out(parts):
    heads, tokens = parts[0][0].shape[:2]
    flat = [array for part in parts for array in part[:3]]
    whole = jax.ShapeDtypeStruct((len(parts) * heads, tokens, HS), jnp.float32)
    return pallas(
        lay_kernel,
        "lay_out",
        [whole, whole],
        in_vmem(len(flat)),
        in_vmem(2),
        [],
    )(*flat)


ROWS = 64


def final_kernel(pairs, target_ref, state_ref, prod_ref, *refs):
    devices = lax.axis_size("seq")
    here = lax.axis_index("seq")
    ends, refs = refs[: devices - 1], refs[devices - 1 :]
    student_ref, loss_ref, ends_s, rows, sem = refs
    tokens, full = rows.shape
    heads = state_ref.shape[0] // len(pairs)
    for apart in range(1, devices):
        ends_s[lax.bitwise_xor(here, apart)] = ends[apart - 1][...]
    places = []
    for slot, pair in enumerate(pairs):
        incoming = jnp.zeros((heads, HS), jnp.float32)
        row = 2 * heads * slot
        for place in range(devices - 1):
            after = ends_s[place, row : row + heads, :] * incoming + (
                ends_s[place, row + heads : row + 2 * heads, :]
            )
            incoming = jnp.where(place < here, after, incoming)
        base = lax.bitwise_xor(lax.axis_index("fsdp"), pair) * heads
        for head in range(heads):
            places.append((slot * heads + head, lanes_of(base + head), incoming[head : head + 1]))
    copies, scales, totals = [], [], []
    for block in range(0, tokens, ROWS):
        at = pl.ds(block, ROWS)
        squares = jnp.zeros((ROWS, HS), jnp.float32)
        for index, lanes, entering in places:
            rounded = (state_ref[index, at, :] + prod_ref[index, at, :] * entering).astype(
                jnp.bfloat16
            )
            rows[at, lanes] = rounded
            value = rounded.astype(jnp.float32)
            squares = squares + value * value
        copies.append(
            pltpu.make_async_copy(rows.at[at, :], student_ref.at[0, at, :], sem.at[len(copies)])
        )
        copies[-1].start()
        mean = jnp.sum(squares, axis=1, keepdims=True) * (1.0 / full)
        scales.append(jnp.broadcast_to(lax.rsqrt(mean + 1e-06), (ROWS, HS)))
    for block, scale in zip(range(0, tokens, ROWS), scales):
        at = pl.ds(block, ROWS)
        total = jnp.zeros((ROWS, HS), jnp.float32)
        for start in range(0, full, HS):
            lanes = slice(start, start + HS)
            wanted = target_ref[0, at, lanes].astype(jnp.float32)
            off = rows[at, lanes].astype(jnp.float32) * scale - wanted
            total = total + off * off
        totals.append(total)
    total = jnp.concatenate(totals, axis=0)
    loss_ref[...] = jnp.sum(total.T, axis=0, keepdims=True) * (1.0 / full)
    for copy in copies:
        copy.wait()


def final(pairs, target, states, products, ends):
    tokens = states.shape[1]
    full = HEADS * HS
    return pallas(
        functools.partial(final_kernel, pairs),
        "final",
        [
            jax.ShapeDtypeStruct((1, tokens, full), jnp.bfloat16),
            jax.ShapeDtypeStruct((1, tokens), jnp.float32),
        ],
        in_vmem(3 + len(ends)),
        [pl.BlockSpec(memory_space=pltpu.HBM)] + in_vmem(1),
        [
            pltpu.VMEM((len(ends) + 1,) + ends[0].shape, jnp.float32),
            pltpu.VMEM((tokens, full), jnp.bfloat16),
            pltpu.SemaphoreType.DMA((tokens // ROWS,)),
        ],
    )(target, states, products, *ends)


def swap(value, axis, apart):
    return lax.ppermute(value, axis, [(i, i ^ apart) for i in range(lax.axis_size(axis))])


def after(value, *earlier):
    return lax.optimization_barrier((value, *earlier))[0]


def local(
    branch_x, positions, teacher_held, gate_weights, gate_bias, conv_weight, conv_bias, decay_rate
):
    tokens, width = branch_x.shape[1:]
    total = lax.axis_size("seq") * tokens
    target = swap(teacher_held, "segment", 1)
    quarter = cut(gate_weights)
    half, edge, *small = fetch(
        branch_x, gate_weights, positions, conv_weight, conv_bias.reshape(1, width)
    )
    quarters = {pair: swap(quarter, "fsdp", pair) for pair in (2, 3)}
    half = swap(half, "fsdp", 1)
    edge = from_behind(edge, "seq", 1)
    conv, masks = conv_rows(branch_x, edge, *small)
    params = (gate_bias, decay_rate.reshape(1, width))
    parts = [shard(conv, masks, params, 0, [gate_weights], total)]
    two = swap(quarters[2], "seq", 2)
    three = swap(after(quarters[3], masks), "seq", 2)
    mine = after(quarters[2], two, parts[0][3])
    weights = [mine, swap(mine, "seq", 1), two, swap(two, "seq", 1)]
    parts.append(shard(conv, masks, params, 2, weights, total))
    half = after(half, two)
    weights = [half, swap(half, "seq", 1)]
    before = [part[3] for part in parts]
    parts.append(shard(conv, masks, params, 1, weights, total, ()))
    mine = after(quarters[3], three)
    weights = [mine, swap(mine, "seq", 1), three, swap(three, "seq", 1)]
    before = [part[3] for part in parts]
    parts.append(shard(conv, masks, params, 3, weights, total, before))
    end = parts[-1][3]
    ends = [swap(end, "seq", apart) for apart in (1, 2, 3)]
    states, products = lay_out(parts)
    return final((0, 2, 1, 3), target, states, products, ends)


def solution(mesh):
    shards, devices = mesh.shape["fsdp"], mesh.shape["seq"]
    whole = shards == 4 and devices == 4
    in_specs = (
        P(("segment", "fsdp"), "seq", None),
        P(("segment", "fsdp"), "seq"),
        P(("segment", "fsdp"), "seq", None),
        P("fsdp", None, None, None),
        P(),
        P(),
        P(),
        P(),
    )
    out_specs = (P(("segment", "fsdp"), "seq", None), P(("segment", "fsdp"), "seq"))
    return jax.shard_map(
        local if whole else general,
        mesh=mesh,
        in_specs=in_specs,
        out_specs=out_specs,
        check_vma=False,
    )
```
